128 devices in a mesh: section: 4 (over z), dp: 4 (over x_hi, core), tensor: 8 (over x_lo, y).
Axes of the slice: x: 4 (x_hi: 2, x_lo: 2; x = x_hi * 2 + x_lo), y: 4, z: 4, core: 2. Of those that a mesh axis runs over, the one named last changes fastest.
Arguments:
- inputs: bfloat16 [8, 128, 8192], P(None, 'dp', ('section', 'tensor')), may hold values from -6 to 6
- gate_wide: bfloat16 [8192, 14336], P('section', 'tensor'), may hold values from -0.0625 to 0.0625
- up_wide: bfloat16 [8192, 14336], P('section', 'tensor'), may hold values from -0.0625 to 0.0625
- down_wide: bfloat16 [14336, 8192], P('tensor', 'section'), may hold values from -0.09375 to 0.09375
- width_wide: int32 [1], replicated, may hold values from 7168 to 14336
- gate_narrow: bfloat16 [8192, 7168], P(('section', 'tensor'), 'dp'), may hold values from -0.0625 to 0.0625
- up_narrow: bfloat16 [8192, 7168], P(('section', 'tensor'), 'dp'), may hold values from -0.0625 to 0.0625
- down_narrow: bfloat16 [7168, 8192], P('dp', ('section', 'tensor')), may hold values from -0.125 to 0.125
- width_narrow: int32 [1], replicated, may hold values from 3584 to 7168
- cotangent: bfloat16 [8, 128, 8192], P('tensor', 'dp', 'section'), may hold values from -6 to 6
Outputs:
- outputs: bfloat16 [8, 128, 8192], P('tensor', 'dp', 'section')
- input_grad: bfloat16 [8, 128, 8192], P(None, 'dp', ('section', 'tensor'))
The draws below stay inside these ranges and needn't reach their ends.
All inputs are finite; a program needn't handle non-finite values.
Results may differ from the reference program's by a relative error of at most 0.017.
Values may be sent and summed in bfloat16 or wider, within the bound.
No kernel may reach another device: no remote copies, remote signals or barrier semaphores. Data moves between devices by JAX's collectives and lax.ppermute only.
A program may use at most 128 MiB of HBM per device.

```python
import jax
import jax.numpy as jnp

D = 8192
FF_A = 14336
FF_B = 7168
TOK_DEV = 128
BLOCKS = 8
TOKENS = 1024


def levels(key, dims, pieces, least, top_value):
    loudness, own = 1.0, jax.random.fold_in(key, 6)
    for dim, shards_of in pieces:
        steps = jnp.exp(jax.random.uniform(jax.random.fold_in(own, dim), (shards_of,), jnp.float32, least / len(pieces), top_value / len(pieces)))
        loudness = loudness * jnp.repeat(steps, dims[dim] // shards_of).reshape([-1 if axis == dim else 1 for axis in range(len(dims))])
    return loudness


def centred(key, shape, scale, bound, split=(), kind=jnp.bfloat16):
    values = jax.random.normal(key, shape, jnp.float32) * scale
    if len(split) > 0:
        values = levels(key, shape, split, -0.22, 0.18) * values
    return jnp.clip(values, min=-bound, max=bound).astype(kind)


def setup_inputs(seed: int = 0) -> dict:
    keys = jax.random.split(jax.random.key(seed), 11)
    return {
        "inputs": centred(keys[0], (BLOCKS, TOK_DEV, D), 1.0, 6.0, ((1, 4), (2, 32))),
        "gate_wide": centred(keys[1], (D, FF_A), D ** -0.5, 0.0625, ((0, 4), (1, 8))),
        "up_wide": centred(keys[2], (D, FF_A), D ** -0.5, 0.0625, ((0, 4), (1, 8))),
        "down_wide": centred(keys[3], (FF_A, D), (FF_A // 4) ** -0.5, 0.09375, ((0, 8), (1, 4))),
        "width_wide": jax.random.randint(keys[4], (1,), FF_A // 2, FF_A + 1).astype(jnp.int32),
        "gate_narrow": centred(keys[5], (D, FF_B), D ** -0.5, 0.0625, ((0, 32), (1, 4))),
        "up_narrow": centred(keys[6], (D, FF_B), D ** -0.5, 0.0625, ((0, 32), (1, 4))),
        "down_narrow": centred(keys[7], (FF_B, D), (FF_B // 4) ** -0.5, 0.125, ((0, 4), (1, 32))),
        "width_narrow": jax.random.randint(keys[8], (1,), FF_B // 2, FF_B + 1).astype(jnp.int32),
        "cotangent": centred(keys[9], (BLOCKS, TOK_DEV, D), 1.0, 6.0, ((0, 8), (1, 4), (2, 4))),
    }


def against(left, weight):
    return jnp.dot(left, weight.T, preferred_element_type=jnp.float32)


def forward_section(values, gate_w, up_w, down_w, width):
    gate = jnp.dot(values, gate_w, preferred_element_type=jnp.float32)
    upper = jnp.dot(values, up_w, preferred_element_type=jnp.float32)
    units = jnp.arange(gate_w.shape[1], dtype=jnp.int32)
    mask = (units < width[0]).astype(jnp.float32)
    sigma = jax.nn.sigmoid(gate)
    hidden = (gate * sigma * upper * mask).astype(jnp.bfloat16)
    result = values.astype(jnp.float32) + jnp.dot(hidden, down_w, preferred_element_type=jnp.float32)
    return result.astype(jnp.bfloat16), gate, upper, mask


def backward_section(grad, gate, upper, mask, gate_w, up_w, down_w):
    dhid = against(grad, down_w)
    sigma = jax.nn.sigmoid(gate)
    dgate = (dhid * upper * sigma * (1.0 + gate * (1.0 - sigma)) * mask).astype(jnp.bfloat16)
    dup = (dhid * gate * sigma * mask).astype(jnp.bfloat16)
    total = grad.astype(jnp.float32) + against(dgate, gate_w) + against(dup, up_w)
    return total.astype(jnp.bfloat16)


def reference(inputs, gate_wide, up_wide, down_wide, width_wide, gate_narrow, up_narrow, down_narrow, width_narrow, cotangent):
    flat = inputs.reshape(TOKENS, D)
    middle, gate_a, upper_a, mask_a = forward_section(flat, gate_wide, up_wide, down_wide, width_wide)
    final, gate_b, upper_b, mask_b = forward_section(middle, gate_narrow, up_narrow, down_narrow, width_narrow)
    middle_grad = backward_section(cotangent.reshape(TOKENS, D), gate_b, upper_b, mask_b, gate_narrow, up_narrow, down_narrow)
    input_grad = backward_section(middle_grad, gate_a, upper_a, mask_a, gate_wide, up_wide, down_wide)
    return final.reshape(BLOCKS, TOK_DEV, D), input_grad.reshape(BLOCKS, TOK_DEV, D)
```

```python
import functools

import jax
import jax.numpy as jnp
from jax import lax
from jax.experimental import pallas as pl
from jax.experimental.pallas import tpu as pltpu
from jax.sharding import PartitionSpec as P

BF = jnp.bfloat16
F32 = jnp.float32
NT = (((1,), (1,)), ((), ()))


def ring(n, shift):
    return [(i, (i + shift) % n) for i in range(n)]


def send(parts, axis, n):
    return [lax.ppermute(p, axis, ring(n, r)) for r, p in zip(range(1, n), parts)]


def spread(own, axis, n):
    return [own] + send([own] * (n - 1), axis, n)


def whole(shape):
    zeros = (0,) * len(shape)
    return pl.BlockSpec(shape, lambda n, idx: zeros)


def fill_features(scratch, refs, t, slot):
    width = refs[0].shape[1]
    for k, ref in enumerate(refs):
        owner = lax.rem(t - k + 8, 8)
        at = pl.multiple_of(slot(owner, t) * width, width)
        scratch[:, pl.ds(at, width)] = ref[...]


def fill_rows(scratch, refs, me, n):
    rows = refs[0].shape[-2]
    for k, ref in enumerate(refs):
        at = pl.multiple_of(lax.rem(me - k + n, n) * rows, rows)
        if len(ref.shape) == 3:
            for g in range(ref.shape[0]):
                scratch[g, pl.ds(at, rows), :] = ref[g]
        else:
            scratch[pl.ds(at, rows), :] = ref[...]


def plain_slot(owner, t):
    return owner


def narrow_slot(owner, t):
    return ((owner ^ t) & 1) * 4 + owner // 2


def out_sections(value_ref, outs, s, place):
    rows = value_ref.shape[0] // 4
    for r, out in enumerate(outs):
        at = pl.multiple_of(lax.rem(s + r, 4) * rows, rows)
        place(out, value_ref[pl.ds(at, rows), :].astype(out.dtype))


def call(kernel, idx, operands, in_specs, out_shape, out_specs, grid, scratch, flops, moved):
    return pl.pallas_call(
        kernel,
        grid_spec=pltpu.PrefetchScalarGridSpec(
            num_scalar_prefetch=1,
            grid=(grid,),
            in_specs=in_specs,
            out_specs=out_specs,
            scratch_shapes=scratch,
        ),
        out_shape=out_shape,
        compiler_params=pltpu.CompilerParams(vmem_limit_bytes=32 << 20),
        cost_estimate=pl.CostEstimate(flops=flops, bytes_accessed=moved, transcendentals=0),
    )(idx, *operands)


def gate_up(idx, chunks, gate_w, up_w, narrow):
    tokens, width = chunks[0].shape
    feats = 8 * width
    units = gate_w.shape[-1]
    block = 128 if narrow else 256
    steps = units // block
    rows = tokens // 4
    mid_rows = tokens // 8

    def kernel(idx_ref, *refs):
        xs, g_ref, u_ref = refs[:8], refs[8], refs[9]
        outs = refs[10:14]
        mid, lhs, val = refs[14], refs[15], refs[16]
        s, t = idx_ref[0], idx_ref[1]

        @pl.when(pl.program_id(0) == 0)
        def _():
            fill_features(lhs, xs, t, narrow_slot if narrow else plain_slot)
            at = pl.multiple_of(t * mid_rows, mid_rows)
            for k, ref in enumerate(xs):
                owner = lax.rem(t - k + 8, 8)
                to = pl.multiple_of(owner * width, width)
                mid[:, pl.ds(to, width)] = ref[pl.ds(at, mid_rows), :]

        if narrow:
            gw = [g_ref[:, j].reshape(feats // 2, block) for j in range(2)]
            uw = [u_ref[:, j].reshape(feats // 2, block) for j in range(2)]
            w = jnp.concatenate(
                [jnp.concatenate(gw, axis=0), jnp.concatenate(uw, axis=0)], axis=1
            )
            val[...] = jnp.dot(lhs[...], w, preferred_element_type=F32)
        else:
            val[:, :block] = jnp.dot(lhs[...], g_ref[...], preferred_element_type=F32)
            val[:, block:] = jnp.dot(lhs[...], u_ref[...], preferred_element_type=F32)

        def place(out, v):
            out[0] = v[:, :block]
            out[1] = v[:, block:]

        out_sections(val, outs, s, place)

    if narrow:
        w_specs = [
            pl.BlockSpec((4, 2, width, block), lambda n, idx: (0, 0, 0, n)),
            pl.BlockSpec((4, 2, width, block), lambda n, idx: (0, 1, 0, n)),
        ]
    else:
        w_specs = [pl.BlockSpec((feats, block), lambda n, idx: (0, n))] * 2
    out_spec = pl.BlockSpec((2, rows, block), lambda n, idx: (0, 0, n))
    res = call(
        kernel,
        idx,
        (*chunks, gate_w, up_w),
        [whole(chunks[0].shape)] * 8 + w_specs,
        [jax.ShapeDtypeStruct((2, rows, units), F32)]
        + [jax.ShapeDtypeStruct((2, rows, units), BF)] * 3
        + [jax.ShapeDtypeStruct((mid_rows, feats), BF)],
        [out_spec] * 4 + [whole((mid_rows, feats))],
        steps,
        [pltpu.VMEM((tokens, feats), BF), pltpu.VMEM((tokens, 2 * block), F32)],
        4 * tokens * feats * units,
        4 * feats * units,
    )
    return res[0], res[1:4], res[4]


def down_wide_part(idx, chunks, down_w):
    rows, units = chunks[0].shape
    tokens = 4 * rows
    feats = down_w.shape[1]
    width = feats // 8

    def kernel(idx_ref, *refs):
        hs, w_ref, outs, lhs = refs[:4], refs[4], refs[5:13], refs[13]
        step = pl.program_id(0)

        @pl.when(step == 0)
        def _():
            fill_rows(lhs, hs, idx_ref[0], 4)

        value = jnp.dot(lhs[...], w_ref[...], preferred_element_type=F32)
        for k in range(8):
            out = outs[k]

            @pl.when(step == (k + 7) % 8)
            def _(out=out):
                out[...] = value.astype(out.dtype)

    res = call(
        kernel,
        idx,
        (*chunks, down_w),
        [whole(chunks[0].shape)] * 4
        + [pl.BlockSpec((units, width), lambda n, idx: (0, lax.rem(idx[1] + n + 1, 8)))],
        [jax.ShapeDtypeStruct((tokens, width), F32)]
        + [jax.ShapeDtypeStruct((tokens, width), BF)] * 7,
        [whole((tokens, width))] * 8,
        8,
        [pltpu.VMEM((tokens, units), BF)],
        2 * tokens * feats * units,
        2 * feats * units,
    )
    return res[0], res[1:]


def down_narrow_part(idx, chunks, down_w):
    rows, units = chunks[0].shape
    tokens = 4 * rows
    width = down_w.shape[-1]
    feats = 8 * width
    mid_rows = tokens // 8

    def kernel(idx_ref, *refs):
        hs, w_ref, outs, lhs, acc = refs[:4], refs[4], refs[5:13], refs[13], refs[14]
        step = pl.program_id(0)
        t = idx_ref[1]

        @pl.when(step == 0)
        def _():
            fill_rows(lhs, hs, idx_ref[0], 4)

        owner = 2 * (step // 2) + ((step & 1) ^ (t & 1))
        at = pl.multiple_of(owner * width, width)
        acc[:, pl.ds(at, width)] = jnp.dot(lhs[...], w_ref[0, 0], preferred_element_type=F32)

        @pl.when(step == 7)
        def _():
            for k, out in enumerate(outs):
                row = pl.multiple_of(lax.rem(t + k, 8) * mid_rows, mid_rows)
                out[...] = acc[pl.ds(row, mid_rows), :].astype(out.dtype)

    res = call(
        kernel,
        idx,
        (*chunks, down_w),
        [whole(chunks[0].shape)] * 4
        + [pl.BlockSpec((1, 1, units, width), lambda n, idx: (n // 2, n & 1, 0, 0))],
        [jax.ShapeDtypeStruct((mid_rows, feats), F32)]
        + [jax.ShapeDtypeStruct((mid_rows, feats), BF)] * 7,
        [whole((mid_rows, feats))] * 8,
        8,
        [pltpu.VMEM((tokens, units), BF), pltpu.VMEM((tokens, feats), F32)],
        2 * tokens * feats * units,
        2 * feats * units,
    )
    return res[0], res[1:]


def hidden_grad_wide(idx, chunks, down_w):
    tokens, width = chunks[0].shape
    feats = 8 * width
    units = down_w.shape[0]
    block = 256
    rows = tokens // 4

    def kernel(idx_ref, *refs):
        xs, w_ref, outs, lhs, val = refs[:8], refs[8], refs[9:13], refs[13], refs[14]
        s, t = idx_ref[0], idx_ref[1]

        @pl.when(pl.program_id(0) == 0)
        def _():
            fill_features(lhs, xs, t, plain_slot)

        val[...] = lax.dot_general(lhs[...], w_ref[...], NT, preferred_element_type=F32)

        def place(out, v):
            out[...] = v

        out_sections(val, outs, s, place)

    res = call(
        kernel,
        idx,
        (*chunks, down_w),
        [whole(chunks[0].shape)] * 8 + [pl.BlockSpec((block, feats), lambda n, idx: (n, 0))],
        [jax.ShapeDtypeStruct((rows, units), F32)]
        + [jax.ShapeDtypeStruct((rows, units), BF)] * 3,
        [pl.BlockSpec((rows, block), lambda n, idx: (0, n))] * 4,
        units // block,
        [pltpu.VMEM((tokens, feats), BF), pltpu.VMEM((tokens, block), F32)],
        2 * tokens * feats * units,
        2 * feats * units,
    )
    return res[0], res[1:]


def hidden_grad_narrow(idx, chunks, down_w):
    mid_rows, feats = chunks[0].shape
    tokens = 8 * mid_rows
    width = feats // 8
    units = down_w.shape[2]
    block = 128
    rows = tokens // 4

    def kernel(idx_ref, *refs):
        xs, w_ref, outs, own, lhs, val = (
            refs[:8], refs[8], refs[9:13], refs[13], refs[14], refs[15],
        )
        s, t = idx_ref[0], idx_ref[1]

        @pl.when(pl.program_id(0) == 0)
        def _():
            fill_rows(lhs, xs, t, 8)
            own[...] = lhs[:, pl.ds(pl.multiple_of(t * width, width), width)]

        total = None
        for f in range(4):
            for j in range(2):
                owner = 2 * f + (j ^ (t & 1))
                left = lhs[:, pl.ds(pl.multiple_of(owner * width, width), width)]
                term = lax.dot_general(left, w_ref[f, j], NT, preferred_element_type=F32)
                total = term if total is None else total + term
        val[...] = total

        def place(out, v):
            out[...] = v

        out_sections(val, outs, s, place)

    res = call(
        kernel,
        idx,
        (*chunks, down_w),
        [whole(chunks[0].shape)] * 8
        + [pl.BlockSpec((4, 2, block, width), lambda n, idx: (0, 0, n, 0))],
        [jax.ShapeDtypeStruct((rows, units), F32)]
        + [jax.ShapeDtypeStruct((rows, units), BF)] * 3
        + [jax.ShapeDtypeStruct((tokens, width), BF)],
        [pl.BlockSpec((rows, block), lambda n, idx: (0, n))] * 4 + [whole((tokens, width))],
        units // block,
        [pltpu.VMEM((tokens, feats), BF), pltpu.VMEM((tokens, block), F32)],
        2 * tokens * feats * units,
        2 * feats * units,
    )
    return res[0], res[1:4], res[4]


def input_back(idx, chunks, gate_w, up_w, narrow):
    _, rows, units = chunks[0].shape
    tokens = 4 * rows
    width = 256
    feats = 8 * width

    def kernel(idx_ref, *refs):
        ps, g_ref, u_ref, outs, lhs = refs[:4], refs[4], refs[5], refs[6:14], refs[14]
        step = pl.program_id(0)

        @pl.when(step == 0)
        def _():
            fill_rows(lhs, ps, idx_ref[0], 4)

        gw = g_ref[0, 0] if narrow else g_ref[...]
        uw = u_ref[0, 0] if narrow else u_ref[...]
        value = lax.dot_general(lhs[0], gw, NT, preferred_element_type=F32)
        value += lax.dot_general(lhs[1], uw, NT, preferred_element_type=F32)
        for k in range(8):
            out = outs[k]

            @pl.when(step == (k + 7) % 8)
            def _(out=out):
                out[...] = value.astype(out.dtype)

    def dest(n, idx):
        return lax.rem(idx[1] + n + 1, 8)

    if narrow:
        w_specs = [
            pl.BlockSpec(
                (1, 1, width, units),
                lambda n, idx: (dest(n, idx) // 2, (dest(n, idx) ^ idx[1]) & 1, 0, 0),
            ),
            pl.BlockSpec(
                (1, 1, width, units),
                lambda n, idx: (dest(n, idx) // 2, 2 + ((dest(n, idx) ^ idx[1]) & 1), 0, 0),
            ),
        ]
    else:
        w_specs = [pl.BlockSpec((width, units), lambda n, idx: (dest(n, idx), 0))] * 2
    res = call(
        kernel,
        idx,
        (*chunks, gate_w, up_w),
        [whole(chunks[0].shape)] * 4 + w_specs,
        [jax.ShapeDtypeStruct((tokens, width), F32)]
        + [jax.ShapeDtypeStruct((tokens, width), BF)] * 7,
        [whole((tokens, width))] * 8,
        8,
        [pltpu.VMEM((2, tokens, units), BF)],
        4 * tokens * feats * units,
        4 * feats * units,
    )
    return res[0], res[1:]


def add_up(own, received):
    total = own
    for r in received:
        total = total + r.astype(F32)
    return total


def hidden_of(gate, upper, mask):
    sigma = jax.nn.sigmoid(gate)
    return (gate * sigma * upper * mask).astype(BF)


def grads_of(dhid, gate, upper, mask):
    sigma = jax.nn.sigmoid(gate)
    dgate = (dhid * upper * sigma * (1.0 + gate * (1.0 - sigma)) * mask).astype(BF)
    dup = (dhid * gate * sigma * mask).astype(BF)
    return jnp.stack([dgate, dup])


def halves(w, axis, tensor):
    size = w.shape[axis] // 2
    parts = []
    for j in range(2):
        half = (tensor & 1) ^ j
        piece = lax.dynamic_slice_in_dim(w, half * size, size, axis)
        perm = [
            (d * 8 + t, (t // 2) * 8 + 2 * d + ((t & 1) ^ j)) for d in range(4) for t in range(8)
        ]
        parts.append(lax.ppermute(piece, ("dp", "tensor"), perm))
    return parts


def body(
    inputs,
    gate_wide,
    up_wide,
    down_wide,
    width_wide,
    gate_narrow,
    up_narrow,
    down_narrow,
    width_narrow,
    cotangent,
):
    section = lax.axis_index("section").astype(jnp.int32)
    tensor = lax.axis_index("tensor").astype(jnp.int32)
    idx = jnp.stack([section, tensor])
    units_a = gate_wide.shape[1]
    units_b = gate_narrow.shape[1] // 2
    mask_a = (
        tensor * units_a + jnp.arange(units_a, dtype=jnp.int32) < width_wide[0]
    ).astype(F32)
    mask_b = (
        tensor * units_b + jnp.arange(units_b, dtype=jnp.int32) < width_narrow[0]
    ).astype(F32)
    blocks, quarter, width = inputs.shape
    tokens = blocks * quarter
    own_in = inputs.reshape(tokens, width)

    x_chunks = spread(own_in, "tensor", 8)
    gu_b = jnp.stack(halves(gate_narrow, 1, tensor) + halves(up_narrow, 1, tensor))
    gu_b = lax.all_gather(gu_b, "dp", axis=0, tiled=False)
    down_b = jnp.stack(halves(down_narrow, 0, tensor))
    down_b = lax.all_gather(down_b, "dp", axis=0, tiled=False)

    own, parts, _ = gate_up(idx, x_chunks, gate_wide, up_wide, False)
    both_a = add_up(own, send(parts, "section", 4))
    hidden_a = hidden_of(both_a[0], both_a[1], mask_a)
    own, parts = down_wide_part(idx, spread(hidden_a, "section", 4), down_wide)
    middle = (own_in.astype(F32) + add_up(own, send(parts, "tensor", 8))).astype(BF)

    own, parts, mid_rows = gate_up(idx, spread(middle, "tensor", 8), gu_b, gu_b, True)
    both_b = add_up(own, send(parts, "section", 4))

    cot_chunks = spread(cotangent[0], "tensor", 8)
    own, parts, cot_own = hidden_grad_narrow(idx, cot_chunks, down_b)
    dhid_b = add_up(own, send(parts, "section", 4))

    pair_b = grads_of(dhid_b, both_b[0], both_b[1], mask_b)
    own, parts = input_back(idx, spread(pair_b, "section", 4), gu_b, gu_b, True)
    middle_grad = (cot_own.astype(F32) + add_up(own, send(parts, "tensor", 8))).astype(BF)

    hidden_b = hidden_of(both_b[0], both_b[1], mask_b)
    own, parts = down_narrow_part(idx, spread(hidden_b, "section", 4), down_b)
    outputs = (mid_rows.astype(F32) + add_up(own, send(parts, "tensor", 8))).astype(BF)

    own, parts = hidden_grad_wide(idx, spread(middle_grad, "tensor", 8), down_wide)
    dhid_a = add_up(own, send(parts, "section", 4))
    pair_a = grads_of(dhid_a, both_a[0], both_a[1], mask_a)
    own, parts = input_back(idx, spread(pair_a, "section", 4), gate_wide, up_wide, False)
    input_grad = (middle_grad.astype(F32) + add_up(own, send(parts, "tensor", 8))).astype(BF)
    return (
        outputs.reshape(1, quarter, outputs.shape[1]),
        input_grad.reshape(blocks, quarter, width),
    )


def solution(mesh):
    in_specs = (
        P(None, "dp", ("section", "tensor")),
        P("section", "tensor"),
        P("section", "tensor"),
        P("tensor", "section"),
        P(),
        P(("section", "tensor"), "dp"),
        P(("section", "tensor"), "dp"),
        P("dp", ("section", "tensor")),
        P(),
        P("tensor", "dp", "section"),
    )
    out_specs = (P("tensor", "dp", "section"), P(None, "dp", ("section", "tensor")))
    return jax.shard_map(body, mesh=mesh, in_specs=in_specs, out_specs=out_specs, check_vma=False)
```

```python
import jax
import jax.numpy as jnp
from jax import lax
from jax.experimental import pallas as pl
from jax.experimental.pallas import tpu as pltpu
from jax.sharding import PartitionSpec as P

BF = jnp.bfloat16
F32 = jnp.float32
VMEM = 8 << 20
NT = (((1,), (1,)), ((), ()))


def ring(n, shift):
    return [(i, (i + shift) % n) for i in range(n)]


def send(parts, axis, n):
    return [lax.ppermute(p, axis, ring(n, r)) for r, p in zip(range(1, n), parts)]


def spread(own, axis, n):
    return [own] + send([own] * (n - 1), axis, n)


VM = pl.BlockSpec(memory_space=pltpu.VMEM)
SM = pl.BlockSpec(memory_space=pltpu.SMEM)


def fill_features(scratch, refs, t, mix, slot):
    width = refs[0].shape[1]
    for k, ref in enumerate(refs):
        owner = lax.rem(t - k + 8, 8)
        at = pl.multiple_of(slot(owner, mix) * width, width)
        scratch[:, pl.ds(at, width)] = ref[...]


def fill_rows(scratch, refs, me, n):
    rows = refs[0].shape[-2]
    for k, ref in enumerate(refs):
        at = pl.multiple_of(lax.rem(me - k + n, n) * rows, rows)
        if len(ref.shape) == 3:
            for g in range(ref.shape[0]):
                scratch[g, pl.ds(at, rows), :] = ref[g]
        else:
            scratch[pl.ds(at, rows), :] = ref[...]


def plain_slot(owner, mix):
    return owner


def narrow_slot(owner, mix):
    return owner ^ mix


def call(kernel, idx, operands, outs, scratch, flops, moved):
    return pl.pallas_call(
        kernel,
        in_specs=[SM] + [VM] * len(operands),
        out_specs=[VM] * len(outs),
        out_shape=[pltpu.VMEM(shape, kind) for shape, kind in outs],
        scratch_shapes=scratch,
        compiler_params=pltpu.CompilerParams(vmem_limit_bytes=VMEM),
        cost_estimate=pl.CostEstimate(flops=flops, bytes_accessed=moved, transcendentals=0),
    )(idx, *operands)


def into_vmem(*weights):
    n = len(weights)

    def kernel(*refs):
        copies = [
            pltpu.make_async_copy(refs[i], refs[n + i], refs[2 * n].at[i]) for i in range(n)
        ]
        for c in copies:
            c.start()
        for c in copies:
            c.wait()

    moved = sum(w.size * 2 for w in weights)
    return pl.pallas_call(
        kernel,
        in_specs=[pl.BlockSpec(memory_space=pltpu.HBM)] * n,
        out_specs=[VM] * n,
        out_shape=[pltpu.VMEM(w.shape, w.dtype) for w in weights],
        scratch_shapes=[pltpu.SemaphoreType.DMA((n,))],
        compiler_params=pltpu.CompilerParams(vmem_limit_bytes=1 << 20),
        cost_estimate=pl.CostEstimate(flops=0, bytes_accessed=2 * moved, transcendentals=0),
    )(*weights)


def gate_up(idx, chunks, weights, narrow):
    tokens, width = chunks[0].shape
    feats = 8 * width
    units = weights[0].shape[-1]
    block = 256
    rows = tokens // 4
    mid_rows = tokens // 8
    n_w = len(weights)

    def kernel(idx_ref, *refs):
        xs, ws = refs[:8], refs[8 : 8 + n_w]
        outs = refs[8 + n_w : 12 + n_w]
        mid, lhs, val = refs[12 + n_w :]
        s, t, mix = idx_ref[0], idx_ref[1], idx_ref[2]
        fill_features(lhs, xs, t, mix, narrow_slot if narrow else plain_slot)
        if narrow:
            row = pl.multiple_of(t * mid_rows, mid_rows)
            for k, ref in enumerate(xs):
                owner = lax.rem(t - k + 8, 8)
                to = pl.multiple_of(owner * width, width)
                mid[:, pl.ds(to, width)] = ref[pl.ds(row, mid_rows), :]
        for g in range(2):
            for at in range(0, units, block):
                size = min(block, units - at)
                if narrow:
                    value = None
                    for j, w in enumerate(ws):
                        term = jnp.dot(
                            lhs[:, j * width : (j + 1) * width],
                            w[g, :, at : at + size],
                            preferred_element_type=F32,
                        )
                        value = term if value is None else value + term
                else:
                    value = jnp.dot(lhs[...], ws[g][:, at : at + size], preferred_element_type=F32)
                val[:, :size] = value
                for r, out in enumerate(outs):
                    row = pl.multiple_of(lax.rem(s + r, 4) * rows, rows)
                    out[g, :, at : at + size] = val[pl.ds(row, rows), :size].astype(out.dtype)

    res = call(
        kernel,
        idx,
        (*chunks, *weights),
        [((2, rows, units), F32)] + [((2, rows, units), BF)] * 3 + [((mid_rows, feats), BF)],
        [pltpu.VMEM((tokens, feats), BF), pltpu.VMEM((tokens, block), F32)],
        4 * tokens * feats * units,
        4 * feats * units,
    )
    return res[0], res[1:4], res[4]


def down_wide_part(idx, chunks, down_w):
    rows, units = chunks[0].shape
    tokens = 4 * rows
    feats = down_w.shape[1]
    width = feats // 8

    def kernel(idx_ref, *refs):
        hs, w, outs, lhs = refs[:4], refs[4], refs[5:13], refs[13]
        fill_rows(lhs, hs, idx_ref[0], 4)
        for k, out in enumerate(outs):
            at = pl.multiple_of(lax.rem(idx_ref[1] + k, 8) * width, width)
            out[...] = jnp.dot(
                lhs[...], w[:, pl.ds(at, width)], preferred_element_type=F32
            ).astype(out.dtype)

    res = call(
        kernel,
        idx,
        (*chunks, down_w),
        [((tokens, width), F32)] + [((tokens, width), BF)] * 7,
        [pltpu.VMEM((tokens, units), BF)],
        2 * tokens * feats * units,
        2 * feats * units,
    )
    return res[0], res[1:]


def down_narrow_part(idx, chunks, weights):
    rows, units = chunks[0].shape
    tokens = 4 * rows
    width = weights[0].shape[-1]
    feats = 8 * width
    mid_rows = tokens // 8

    def kernel(idx_ref, *refs):
        hs, ws, outs, lhs, acc = refs[:4], refs[4:12], refs[12:20], refs[20], refs[21]
        t, mix = idx_ref[1], idx_ref[2]
        fill_rows(lhs, hs, idx_ref[0], 4)
        for j, w in enumerate(ws):
            at = pl.multiple_of((mix ^ j) * width, width)
            acc[:, pl.ds(at, width)] = jnp.dot(lhs[...], w[...], preferred_element_type=F32)
        for k, out in enumerate(outs):
            row = pl.multiple_of(lax.rem(t + k, 8) * mid_rows, mid_rows)
            out[...] = acc[pl.ds(row, mid_rows), :].astype(out.dtype)

    res = call(
        kernel,
        idx,
        (*chunks, *weights),
        [((mid_rows, feats), F32)] + [((mid_rows, feats), BF)] * 7,
        [pltpu.VMEM((tokens, units), BF), pltpu.VMEM((tokens, feats), F32)],
        2 * tokens * feats * units,
        2 * feats * units,
    )
    return res[0], res[1:]


def hidden_grad_wide(idx, chunks, down_w):
    tokens, width = chunks[0].shape
    feats = 8 * width
    units = down_w.shape[0]
    block = 256
    rows = tokens // 4

    def kernel(idx_ref, *refs):
        xs, w, outs, lhs, val = refs[:8], refs[8], refs[9:13], refs[13], refs[14]
        s, t = idx_ref[0], idx_ref[1]
        fill_features(lhs, xs, t, 0, plain_slot)
        for at in range(0, units, block):
            val[...] = lax.dot_general(
                lhs[...], w[at : at + block, :], NT, preferred_element_type=F32
            )
            for r, out in enumerate(outs):
                row = pl.multiple_of(lax.rem(s + r, 4) * rows, rows)
                out[:, at : at + block] = val[pl.ds(row, rows), :].astype(out.dtype)

    res = call(
        kernel,
        idx,
        (*chunks, down_w),
        [((rows, units), F32)] + [((rows, units), BF)] * 3,
        [pltpu.VMEM((tokens, feats), BF), pltpu.VMEM((tokens, block), F32)],
        2 * tokens * feats * units,
        2 * feats * units,
    )
    return res[0], res[1:]


def hidden_grad_narrow(idx, chunks, weights):
    mid_rows, feats = chunks[0].shape
    tokens = 8 * mid_rows
    width = feats // 8
    units = weights[0].shape[0]
    block = 256
    rows = tokens // 4

    def kernel(idx_ref, *refs):
        xs, ws, outs = refs[:8], refs[8:16], refs[16:20]
        own, lhs, val = refs[20:]
        s, t, mix = idx_ref[0], idx_ref[1], idx_ref[2]
        fill_rows(lhs, xs, t, 8)
        own[...] = lhs[:, pl.ds(pl.multiple_of(t * width, width), width)]
        for at in range(0, units, block):
            size = min(block, units - at)
            total = None
            for j, w in enumerate(ws):
                left = lhs[:, pl.ds(pl.multiple_of((mix ^ j) * width, width), width)]
                term = lax.dot_general(
                    left, w[at : at + size, :], NT, preferred_element_type=F32
                )
                total = term if total is None else total + term
            val[:, :size] = total
            for r, out in enumerate(outs):
                row = pl.multiple_of(lax.rem(s + r, 4) * rows, rows)
                out[:, at : at + size] = val[pl.ds(row, rows), :size].astype(out.dtype)

    res = call(
        kernel,
        idx,
        (*chunks, *weights),
        [((rows, units), F32)] + [((rows, units), BF)] * 3 + [((tokens, width), BF)],
        [pltpu.VMEM((tokens, feats), BF), pltpu.VMEM((tokens, block), F32)],
        2 * tokens * feats * units,
        2 * feats * units,
    )
    return res[0], res[1:4], res[4]


def input_back_wide(idx, chunks, gate_w, up_w):
    _, rows, units = chunks[0].shape
    tokens = 4 * rows
    width = gate_w.shape[0] // 8
    feats = 8 * width

    def kernel(idx_ref, *refs):
        ps, g, u, outs, lhs = refs[:4], refs[4], refs[5], refs[6:14], refs[14]
        fill_rows(lhs, ps, idx_ref[0], 4)
        for k, out in enumerate(outs):
            at = pl.multiple_of(lax.rem(idx_ref[1] + k, 8) * width, width)
            value = lax.dot_general(
                lhs[0], g[pl.ds(at, width), :], NT, preferred_element_type=F32
            )
            value += lax.dot_general(
                lhs[1], u[pl.ds(at, width), :], NT, preferred_element_type=F32
            )
            out[...] = value.astype(out.dtype)

    res = call(
        kernel,
        idx,
        (*chunks, gate_w, up_w),
        [((tokens, width), F32)] + [((tokens, width), BF)] * 7,
        [pltpu.VMEM((2, tokens, units), BF)],
        4 * tokens * feats * units,
        4 * feats * units,
    )
    return res[0], res[1:]


def input_back_narrow(idx, chunks, weights):
    _, rows, units = chunks[0].shape
    tokens = 4 * rows
    width = weights[0].shape[1]
    feats = 8 * width

    def kernel(idx_ref, *refs):
        ps, ws, outs, lhs, acc = refs[:4], refs[4:12], refs[12:20], refs[20], refs[21]
        t, mix = idx_ref[1], idx_ref[2]
        fill_rows(lhs, ps, idx_ref[0], 4)
        for j, w in enumerate(ws):
            value = lax.dot_general(lhs[0], w[0], NT, preferred_element_type=F32)
            value += lax.dot_general(lhs[1], w[1], NT, preferred_element_type=F32)
            acc[mix ^ j] = value
        for k, out in enumerate(outs):
            out[...] = acc[lax.rem(t + k, 8)].astype(out.dtype)

    res = call(
        kernel,
        idx,
        (*chunks, *weights),
        [((tokens, width), F32)] + [((tokens, width), BF)] * 7,
        [pltpu.VMEM((2, tokens, units), BF), pltpu.VMEM((8, tokens, width), F32)],
        4 * tokens * feats * units,
        4 * feats * units,
    )
    return res[0], res[1:]


def add_up(own, received):
    total = own
    for r in received:
        total = total + r.astype(F32)
    return total


def hidden_of(gate, upper, mask):
    sigma = jax.nn.sigmoid(gate)
    return (gate * sigma * upper * mask).astype(BF)


def grads_of(dhid, gate, upper, mask):
    sigma = jax.nn.sigmoid(gate)
    dgate = (dhid * upper * sigma * (1.0 + gate * (1.0 - sigma)) * mask).astype(BF)
    dup = (dhid * gate * sigma * mask).astype(BF)
    return jnp.stack([dgate, dup])


def after(value, *earlier):
    return lax.optimization_barrier((value, earlier))[0]


CORES = [(0, 1), (1, 0), (2, 3), (3, 2)]


def own_half(w, axis, tensor, flip):
    size = w.shape[axis] // 2
    return lax.dynamic_slice_in_dim(w, ((tensor & 1) ^ flip) * size, size, axis)


def hand_out(piece, flip_x, flip_half):
    perm = [
        (
            d * 8 + t,
            ((((t >> 1) & 1) ^ flip_x) * 2 + (t >> 2)) * 8 + 2 * d + ((t & 1) ^ flip_half),
        )
        for d in range(4)
        for t in range(8)
    ]
    return lax.ppermute(piece, ("dp", "tensor"), perm)


def to_sibling(pieces):
    return [lax.ppermute(p, "dp", CORES) for p in pieces]


def body(
    inputs,
    gate_wide,
    up_wide,
    down_wide,
    width_wide,
    gate_narrow,
    up_narrow,
    down_narrow,
    width_narrow,
    cotangent,
):
    section = lax.axis_index("section").astype(jnp.int32)
    tensor = lax.axis_index("tensor").astype(jnp.int32)
    dp = lax.axis_index("dp").astype(jnp.int32)
    mix = (dp & 1) * 4 + (dp >> 1) * 2 + (tensor & 1)
    idx = jnp.stack([section, tensor, mix])
    units_a = gate_wide.shape[1]
    units_b = gate_narrow.shape[1] // 2
    mask_a = (
        tensor * units_a + jnp.arange(units_a, dtype=jnp.int32) < width_wide[0]
    ).astype(F32)
    mask_b = (
        tensor * units_b + jnp.arange(units_b, dtype=jnp.int32) < width_narrow[0]
    ).astype(F32)
    blocks, quarter, width = inputs.shape
    tokens = blocks * quarter
    own_in = inputs.reshape(tokens, width)

    gu_half = [
        jnp.stack([own_half(gate_narrow, 1, tensor, j), own_half(up_narrow, 1, tensor, j)])
        for j in range(2)
    ]
    down_half = [own_half(down_narrow, 0, tensor, j) for j in range(2)]

    gate_wide, up_wide, down_wide = into_vmem(gate_wide, up_wide, down_wide)
    x_chunks = spread(own_in, "tensor", 8)
    first = [hand_out(after(gu_half[j], x_chunks), 0, j) for j in range(2)]
    second = [hand_out(after(gu_half[j], first), 1, j) for j in range(2)]
    gu_b = first + second
    gu_b = gu_b + to_sibling(gu_b)

    own, parts, _ = gate_up(idx, x_chunks, (gate_wide, up_wide), False)
    both_a = add_up(own, after(send(parts, "section", 4), first))
    hidden_a = hidden_of(both_a[0], both_a[1], mask_a)
    own, parts = down_wide_part(idx, spread(hidden_a, "section", 4), down_wide)
    parts = after(parts, second)
    middle = (own_in.astype(F32) + add_up(own, send(parts, "tensor", 8))).astype(BF)

    mid_chunks = spread(middle, "tensor", 8)
    first = [hand_out(after(down_half[j], mid_chunks), 0, j) for j in range(2)]
    second = [hand_out(after(down_half[j], first), 1, j) for j in range(2)]
    down_b = first + second
    down_b = down_b + to_sibling(down_b)
    own, parts, mid_rows = gate_up(idx, mid_chunks, gu_b, True)
    both_b = add_up(own, send(parts, "section", 4))

    cot_chunks = spread(after(cotangent[0], mid_chunks), "tensor", 8)
    own, parts, cot_own = hidden_grad_narrow(idx, cot_chunks, down_b)
    dhid_b = add_up(own, send(parts, "section", 4))

    pair_b = grads_of(dhid_b, both_b[0], both_b[1], mask_b)
    own, parts = input_back_narrow(idx, spread(pair_b, "section", 4), gu_b)
    middle_grad = (cot_own.astype(F32) + add_up(own, send(parts, "tensor", 8))).astype(BF)
    grad_chunks = spread(middle_grad, "tensor", 8)

    hidden_b = after(hidden_of(both_b[0], both_b[1], mask_b), grad_chunks)
    own, parts = down_narrow_part(idx, spread(hidden_b, "section", 4), down_b)
    outputs = (mid_rows.astype(F32) + add_up(own, send(parts, "tensor", 8))).astype(BF)

    own, parts = hidden_grad_wide(idx, grad_chunks, down_wide)
    dhid_a = add_up(own, send(parts, "section", 4))
    pair_a = grads_of(dhid_a, both_a[0], both_a[1], mask_a)
    own, parts = input_back_wide(idx, spread(pair_a, "section", 4), gate_wide, up_wide)
    input_grad = (middle_grad.astype(F32) + add_up(own, send(parts, "tensor", 8))).astype(BF)
    return (
        outputs.reshape(1, quarter, outputs.shape[1]),
        input_grad.reshape(blocks, quarter, width),
    )


def solution(mesh):
    in_specs = (
        P(None, "dp", ("section", "tensor")),
        P("section", "tensor"),
        P("section", "tensor"),
        P("tensor", "section"),
        P(),
        P(("section", "tensor"), "dp"),
        P(("section", "tensor"), "dp"),
        P("dp", ("section", "tensor")),
        P(),
        P("tensor", "dp", "section"),
    )
    out_specs = (P("tensor", "dp", "section"), P(None, "dp", ("section", "tensor")))
    return jax.shard_map(body, mesh=mesh, in_specs=in_specs, out_specs=out_specs, check_vma=False)
```

```python
import jax
import jax.numpy as jnp
from jax import lax
from jax.experimental import pallas as pl
from jax.experimental.pallas import tpu as pltpu
from jax.sharding import PartitionSpec as P

BF = jnp.bfloat16
F32 = jnp.float32
VMEM = 8 << 20
NT = (((1,), (1,)), ((), ()))


def ring(n, shift):
    return [(i, (i + shift) % n) for i in range(n)]


def send(parts, axis, n):
    return [lax.ppermute(p, axis, ring(n, r)) for r, p in zip(range(1, n), parts)]


def spread(own, axis, n):
    return [own] + send([own] * (n - 1), axis, n)


VM = pl.BlockSpec(memory_space=pltpu.VMEM)
SM = pl.BlockSpec(memory_space=pltpu.SMEM)


def fill_features(scratch, refs, t, mix, slot):
    width = refs[0].shape[1]
    for k, ref in enumerate(refs):
        owner = lax.rem(t - k + 8, 8)
        at = pl.multiple_of(slot(owner, mix) * width, width)
        scratch[:, pl.ds(at, width)] = ref[...]


def fill_rows(scratch, refs, me, n):
    rows = refs[0].shape[-2]
    for k, ref in enumerate(refs):
        at = pl.multiple_of(lax.rem(me - k + n, n) * rows, rows)
        if len(ref.shape) == 3:
            for g in range(ref.shape[0]):
                scratch[g, pl.ds(at, rows), :] = ref[g]
        else:
            scratch[pl.ds(at, rows), :] = ref[...]


def plain_slot(owner, mix):
    return owner


def narrow_slot(owner, mix):
    return (((owner & 1) << 2) | (owner >> 1)) ^ mix


def narrow_owner(slot, mix):
    swapped = slot ^ mix
    return ((swapped & 3) << 1) | (swapped >> 2)


def call(kernel, idx, operands, outs, scratch, flops, moved):
    return pl.pallas_call(
        kernel,
        in_specs=[SM] + [VM] * len(operands),
        out_specs=[VM] * len(outs),
        out_shape=[pltpu.VMEM(shape, kind) for shape, kind in outs],
        scratch_shapes=scratch,
        compiler_params=pltpu.CompilerParams(vmem_limit_bytes=VMEM),
        cost_estimate=pl.CostEstimate(flops=flops, bytes_accessed=moved, transcendentals=0),
    )(idx, *operands)


def into_vmem(*weights):
    n = len(weights)

    def kernel(*refs):
        copies = [
            pltpu.make_async_copy(refs[i], refs[n + i], refs[2 * n].at[i]) for i in range(n)
        ]
        for c in copies:
            c.start()
        for c in copies:
            c.wait()

    moved = sum(w.size * 2 for w in weights)
    return pl.pallas_call(
        kernel,
        in_specs=[pl.BlockSpec(memory_space=pltpu.HBM)] * n,
        out_specs=[VM] * n,
        out_shape=[pltpu.VMEM(w.shape, w.dtype) for w in weights],
        scratch_shapes=[pltpu.SemaphoreType.DMA((n,))],
        compiler_params=pltpu.CompilerParams(vmem_limit_bytes=1 << 20),
        cost_estimate=pl.CostEstimate(flops=0, bytes_accessed=2 * moved, transcendentals=0),
    )(*weights)


def gate_up(idx, chunks, weights, narrow):
    tokens, width = chunks[0].shape
    feats = 8 * width
    units = weights[0].shape[-1]
    block = 256
    rows = tokens // 4
    mid_rows = tokens // 8
    n_w = len(weights)

    def kernel(idx_ref, *refs):
        xs, ws = refs[:8], refs[8 : 8 + n_w]
        outs = refs[8 + n_w : 12 + n_w]
        mid, lhs, val = refs[12 + n_w :]
        s, t, mix = idx_ref[0], idx_ref[1], idx_ref[2]
        fill_features(lhs, xs, t, mix, narrow_slot if narrow else plain_slot)
        if narrow:
            row = pl.multiple_of(t * mid_rows, mid_rows)
            for k, ref in enumerate(xs):
                owner = lax.rem(t - k + 8, 8)
                to = pl.multiple_of(owner * width, width)
                mid[:, pl.ds(to, width)] = ref[pl.ds(row, mid_rows), :]
        for g in range(2):
            for at in range(0, units, block):
                size = min(block, units - at)
                if narrow:
                    value = None
                    for j, w in enumerate(ws):
                        term = jnp.dot(
                            lhs[:, j * width : (j + 1) * width],
                            w[g, :, at : at + size],
                            preferred_element_type=F32,
                        )
                        value = term if value is None else value + term
                else:
                    value = jnp.dot(lhs[...], ws[g][:, at : at + size], preferred_element_type=F32)
                val[:, :size] = value
                for r, out in enumerate(outs):
                    row = pl.multiple_of(lax.rem(s + r, 4) * rows, rows)
                    out[g, :, at : at + size] = val[pl.ds(row, rows), :size].astype(out.dtype)

    res = call(
        kernel,
        idx,
        (*chunks, *weights),
        [((2, rows, units), F32)] + [((2, rows, units), BF)] * 3 + [((mid_rows, feats), BF)],
        [pltpu.VMEM((tokens, feats), BF), pltpu.VMEM((tokens, block), F32)],
        4 * tokens * feats * units,
        4 * feats * units,
    )
    return res[0], res[1:4], res[4]


def down_wide_part(idx, chunks, down_w):
    rows, units = chunks[0].shape
    tokens = 4 * rows
    feats = down_w.shape[1]
    width = feats // 8

    def kernel(idx_ref, *refs):
        hs, w, outs, lhs = refs[:4], refs[4], refs[5:13], refs[13]
        fill_rows(lhs, hs, idx_ref[0], 4)
        for k, out in enumerate(outs):
            at = pl.multiple_of(lax.rem(idx_ref[1] + k, 8) * width, width)
            out[...] = jnp.dot(
                lhs[...], w[:, pl.ds(at, width)], preferred_element_type=F32
            ).astype(out.dtype)

    res = call(
        kernel,
        idx,
        (*chunks, down_w),
        [((tokens, width), F32)] + [((tokens, width), BF)] * 7,
        [pltpu.VMEM((tokens, units), BF)],
        2 * tokens * feats * units,
        2 * feats * units,
    )
    return res[0], res[1:]


def down_narrow_part(idx, chunks, weights):
    rows, units = chunks[0].shape
    tokens = 4 * rows
    width = weights[0].shape[-1]
    feats = 8 * width

    def kernel(idx_ref, *refs):
        hs, ws, out, lhs = refs[:4], refs[4:12], refs[12], refs[13]
        mix = idx_ref[2]
        fill_rows(lhs, hs, idx_ref[0], 4)
        for j, w in enumerate(ws):
            at = pl.multiple_of(narrow_owner(j, mix) * width, width)
            out[:, pl.ds(at, width)] = jnp.dot(lhs[...], w[...], preferred_element_type=F32)

    return call(
        kernel,
        idx,
        (*chunks, *weights),
        [((tokens, feats), F32)],
        [pltpu.VMEM((tokens, units), BF)],
        2 * tokens * feats * units,
        2 * feats * units,
    )[0]


def hidden_grad_wide(idx, chunks, down_w):
    tokens, width = chunks[0].shape
    feats = 8 * width
    units = down_w.shape[0]
    block = 256
    rows = tokens // 4

    def kernel(idx_ref, *refs):
        xs, w, outs, lhs, val = refs[:8], refs[8], refs[9:13], refs[13], refs[14]
        s, t = idx_ref[0], idx_ref[1]
        fill_features(lhs, xs, t, 0, plain_slot)
        for at in range(0, units, block):
            val[...] = lax.dot_general(
                lhs[...], w[at : at + block, :], NT, preferred_element_type=F32
            )
            for r, out in enumerate(outs):
                row = pl.multiple_of(lax.rem(s + r, 4) * rows, rows)
                out[:, at : at + block] = val[pl.ds(row, rows), :].astype(out.dtype)

    res = call(
        kernel,
        idx,
        (*chunks, down_w),
        [((rows, units), F32)] + [((rows, units), BF)] * 3,
        [pltpu.VMEM((tokens, feats), BF), pltpu.VMEM((tokens, block), F32)],
        2 * tokens * feats * units,
        2 * feats * units,
    )
    return res[0], res[1:]


def hidden_grad_narrow(idx, cot, weights):
    tokens, feats = cot.shape
    width = feats // 8
    units = weights[0].shape[0]
    block = 256
    rows = tokens // 4

    def kernel(idx_ref, *refs):
        lhs, ws, outs = refs[0], refs[1:9], refs[9:13]
        own, val = refs[13:]
        s, t, mix = idx_ref[0], idx_ref[1], idx_ref[2]
        own[...] = lhs[:, pl.ds(pl.multiple_of(t * width, width), width)]
        for at in range(0, units, block):
            size = min(block, units - at)
            total = None
            for j, w in enumerate(ws):
                left = lhs[:, pl.ds(pl.multiple_of(narrow_owner(j, mix) * width, width), width)]
                term = lax.dot_general(
                    left, w[at : at + size, :], NT, preferred_element_type=F32
                )
                total = term if total is None else total + term
            val[:, :size] = total
            for r, out in enumerate(outs):
                row = pl.multiple_of(lax.rem(s + r, 4) * rows, rows)
                out[:, at : at + size] = val[pl.ds(row, rows), :size].astype(out.dtype)

    res = call(
        kernel,
        idx,
        (cot, *weights),
        [((rows, units), F32)] + [((rows, units), BF)] * 3 + [((tokens, width), BF)],
        [pltpu.VMEM((tokens, block), F32)],
        2 * tokens * feats * units,
        2 * feats * units,
    )
    return res[0], res[1:4], res[4]


def input_back_wide(idx, chunks, gate_w, up_w):
    _, rows, units = chunks[0].shape
    tokens = 4 * rows
    width = gate_w.shape[0] // 8
    feats = 8 * width

    def kernel(idx_ref, *refs):
        ps, g, u, outs, lhs = refs[:4], refs[4], refs[5], refs[6:14], refs[14]
        fill_rows(lhs, ps, idx_ref[0], 4)
        for k, out in enumerate(outs):
            at = pl.multiple_of(lax.rem(idx_ref[1] + k, 8) * width, width)
            value = lax.dot_general(
                lhs[0], g[pl.ds(at, width), :], NT, preferred_element_type=F32
            )
            value += lax.dot_general(
                lhs[1], u[pl.ds(at, width), :], NT, preferred_element_type=F32
            )
            out[...] = value.astype(out.dtype)

    res = call(
        kernel,
        idx,
        (*chunks, gate_w, up_w),
        [((tokens, width), F32)] + [((tokens, width), BF)] * 7,
        [pltpu.VMEM((2, tokens, units), BF)],
        4 * tokens * feats * units,
        4 * feats * units,
    )
    return res[0], res[1:]


def input_back_narrow(idx, chunks, weights):
    _, rows, units = chunks[0].shape
    tokens = 4 * rows
    width = weights[0].shape[1]
    feats = 8 * width

    def kernel(idx_ref, *refs):
        ps, ws, outs, lhs, acc = refs[:4], refs[4:12], refs[12:20], refs[20], refs[21]
        t, mix = idx_ref[1], idx_ref[2]
        fill_rows(lhs, ps, idx_ref[0], 4)
        for j, w in enumerate(ws):
            value = lax.dot_general(lhs[0], w[0], NT, preferred_element_type=F32)
            value += lax.dot_general(lhs[1], w[1], NT, preferred_element_type=F32)
            acc[narrow_owner(j, mix)] = value
        for k, out in enumerate(outs):
            out[...] = acc[lax.rem(t + k, 8)].astype(out.dtype)

    res = call(
        kernel,
        idx,
        (*chunks, *weights),
        [((tokens, width), F32)] + [((tokens, width), BF)] * 7,
        [pltpu.VMEM((2, tokens, units), BF), pltpu.VMEM((8, tokens, width), F32)],
        4 * tokens * feats * units,
        4 * feats * units,
    )
    return res[0], res[1:]


def add_up(own, received):
    total = own
    for r in received:
        total = total + r.astype(F32)
    return total


def hidden_of(gate, upper, mask):
    sigma = jax.nn.sigmoid(gate)
    return (gate * sigma * upper * mask).astype(BF)


def grads_of(dhid, gate, upper, mask):
    sigma = jax.nn.sigmoid(gate)
    dgate = (dhid * upper * sigma * (1.0 + gate * (1.0 - sigma)) * mask).astype(BF)
    dup = (dhid * gate * sigma * mask).astype(BF)
    return jnp.stack([dgate, dup])


def after(value, *earlier):
    return lax.optimization_barrier((value, earlier))[0]


CORES = [(0, 1), (1, 0), (2, 3), (3, 2)]


def own_half(w, axis, tensor, flip):
    size = w.shape[axis] // 2
    return lax.dynamic_slice_in_dim(w, (((tensor >> 1) & 1) ^ flip) * size, size, axis)


def hand_out(piece, flip_x, flip_half):
    perm = []
    for d in range(4):
        for t in range(8):
            g, a, b = t >> 2, (t >> 1) & 1, t & 1
            to_d = (g ^ flip_x) * 2 + b
            to_t = 4 * (d & 1) + 2 * (d >> 1) + (a ^ flip_half)
            perm.append((d * 8 + t, to_d * 8 + to_t))
    return lax.ppermute(piece, ("dp", "tensor"), perm)


def to_sibling(pieces):
    return [lax.ppermute(p, "dp", CORES) for p in pieces]


def body(
    inputs,
    gate_wide,
    up_wide,
    down_wide,
    width_wide,
    gate_narrow,
    up_narrow,
    down_narrow,
    width_narrow,
    cotangent,
):
    section = lax.axis_index("section").astype(jnp.int32)
    tensor = lax.axis_index("tensor").astype(jnp.int32)
    dp = lax.axis_index("dp").astype(jnp.int32)
    mix = (dp & 1) * 4 + (dp >> 1) * 2 + (tensor & 1)
    idx = jnp.stack([section, tensor, mix])
    units_a = gate_wide.shape[1]
    units_b = gate_narrow.shape[1] // 2
    mask_a = (
        tensor * units_a + jnp.arange(units_a, dtype=jnp.int32) < width_wide[0]
    ).astype(F32)
    from_dp = 2 * ((tensor >> 1) & 1) + (tensor >> 2)
    mask_b = (
        (2 * from_dp + (tensor & 1)) * units_b + jnp.arange(units_b, dtype=jnp.int32) < width_narrow[0]
    ).astype(F32)
    blocks, quarter, width = inputs.shape
    tokens = blocks * quarter
    own_in = inputs.reshape(tokens, width)

    gu_half = [
        jnp.stack([own_half(gate_narrow, 1, tensor, j), own_half(up_narrow, 1, tensor, j)])
        for j in range(2)
    ]
    down_half = [own_half(down_narrow, 0, tensor, j) for j in range(2)]

    cot_rows = lax.all_gather(cotangent[0], "tensor", axis=0, tiled=True)
    x_chunks = spread(own_in, "tensor", 8)
    gate_1, up_1 = into_vmem(*after((gate_wide, up_wide), x_chunks[1], x_chunks[2]))
    ready = after(gu_half, x_chunks)
    a00, a11 = hand_out(ready[0], 0, 0), hand_out(ready[1], 1, 1)
    ready = after(gu_half, (a00, a11))
    a01, a10 = hand_out(ready[1], 0, 1), hand_out(ready[0], 1, 0)
    s00, s11 = to_sibling([a00, a11])

    own, parts, _ = gate_up(idx, x_chunks, (gate_1, up_1), False)
    down_1, = into_vmem(after(down_wide, own))
    both_a = add_up(own, after(send(parts, "section", 4), (a00, a11)))
    hidden_a = hidden_of(both_a[0], both_a[1], mask_a)
    own, parts = down_wide_part(idx, spread(hidden_a, "section", 4), down_1)
    parts = after(parts, (a01, a10, s00, s11, cot_rows))
    middle = (own_in.astype(F32) + add_up(own, send(parts, "tensor", 8))).astype(BF)

    mid_chunks = spread(middle, "tensor", 8)
    s01, s10 = to_sibling(after([a01, a10], mid_chunks))
    gu_b = [a00, a01, a10, a11, s00, s01, s10, s11]
    ready = after(down_half, (s01, s10))
    b00, b11 = hand_out(ready[0], 0, 0), hand_out(ready[1], 1, 1)
    own, parts, mid_rows = gate_up(idx, mid_chunks, gu_b, True)
    ready = after(down_half, own)
    b01, b10 = hand_out(ready[1], 0, 1), hand_out(ready[0], 1, 0)
    down_b = [b00, b01, b10, b11]
    down_b = down_b + to_sibling(down_b)
    both_b = add_up(own, send(parts, "section", 4))

    own, parts, cot_own = hidden_grad_narrow(idx, cot_rows, down_b)
    dhid_b = add_up(own, send(parts, "section", 4))

    pair_b = grads_of(dhid_b, both_b[0], both_b[1], mask_b)
    own, parts = input_back_narrow(idx, spread(pair_b, "section", 4), gu_b)
    middle_grad = (cot_own.astype(F32) + add_up(own, send(parts, "tensor", 8))).astype(BF)
    grad_chunks = spread(middle_grad, "tensor", 8)
    down_2, = into_vmem(after(down_wide, grad_chunks[1], grad_chunks[2]))

    own, parts = hidden_grad_wide(idx, grad_chunks, down_2)

    hidden_b = after(hidden_of(both_b[0], both_b[1], mask_b), middle_grad)
    out_part = down_narrow_part(idx, spread(hidden_b, "section", 4), down_b)
    out_part = after(out_part, own)
    out_sum = lax.psum_scatter(out_part, "tensor", scatter_dimension=0, tiled=True)
    outputs = (mid_rows.astype(F32) + out_sum).astype(BF)

    gate_2, up_2 = into_vmem(*after((gate_wide, up_wide), own))
    dhid_a = add_up(own, send(parts, "section", 4))
    pair_a = grads_of(dhid_a, both_a[0], both_a[1], mask_a)
    own, parts = input_back_wide(idx, spread(pair_a, "section", 4), gate_2, up_2)
    input_grad = (middle_grad.astype(F32) + add_up(own, send(parts, "tensor", 8))).astype(BF)
    return (
        outputs.reshape(1, quarter, outputs.shape[1]),
        input_grad.reshape(blocks, quarter, width),
    )


def solution(mesh):
    in_specs = (
        P(None, "dp", ("section", "tensor")),
        P("section", "tensor"),
        P("section", "tensor"),
        P("tensor", "section"),
        P(),
        P(("section", "tensor"), "dp"),
        P(("section", "tensor"), "dp"),
        P("dp", ("section", "tensor")),
        P(),
        P("tensor", "dp", "section"),
    )
    out_specs = (P("tensor", "dp", "section"), P(None, "dp", ("section", "tensor")))
    return jax.shard_map(body, mesh=mesh, in_specs=in_specs, out_specs=out_specs, check_vma=False)
```

```python
import jax
import jax.numpy as jnp
from jax import lax
from jax.experimental import pallas as pl
from jax.experimental.pallas import tpu as pltpu
from jax.sharding import PartitionSpec as P

BF = jnp.bfloat16
F32 = jnp.float32
VMEM = 8 << 20
NT = (((1,), (1,)), ((), ()))


def ring(n, shift):
    return [(i, (i + shift) % n) for i in range(n)]


def send(parts, axis, n):
    return [lax.ppermute(p, axis, ring(n, r)) for r, p in zip(range(1, n), parts)]


def spread(own, axis, n):
    return [own] + send([own] * (n - 1), axis, n)


VM = pl.BlockSpec(memory_space=pltpu.VMEM)
SM = pl.BlockSpec(memory_space=pltpu.SMEM)


def fill_features(scratch, refs, t, mix, slot):
    width = refs[0].shape[1]
    for k, ref in enumerate(refs):
        owner = lax.rem(t - k + 8, 8)
        at = pl.multiple_of(slot(owner, mix) * width, width)
        scratch[:, pl.ds(at, width)] = ref[...]


def fill_rows(scratch, refs, me, n):
    rows = refs[0].shape[-2]
    for k, ref in enumerate(refs):
        at = pl.multiple_of(lax.rem(me - k + n, n) * rows, rows)
        if len(ref.shape) == 3:
            for g in range(2):
                scratch[g, pl.ds(at, rows), :] = ref[g]
        else:
            scratch[pl.ds(at, rows), :] = ref[...]


def plain_slot(owner, mix):
    return owner


def narrow_slot(owner, mix):
    return (((owner & 1) << 2) | (owner >> 1)) ^ mix


def narrow_owner(slot, mix):
    swapped = slot ^ mix
    return ((swapped & 3) << 1) | (swapped >> 2)


def call(kernel, idx, operands, outs, scratch, flops, moved):
    return pl.pallas_call(
        kernel,
        in_specs=[SM] + [VM] * len(operands),
        out_specs=[VM] * len(outs),
        out_shape=[pltpu.VMEM(shape, kind) for shape, kind in outs],
        scratch_shapes=scratch,
        compiler_params=pltpu.CompilerParams(vmem_limit_bytes=VMEM),
        cost_estimate=pl.CostEstimate(flops=flops, bytes_accessed=moved, transcendentals=0),
    )(idx, *operands)


def into_vmem(*weights):
    n = len(weights)

    def kernel(*refs):
        copies = [
            pltpu.make_async_copy(refs[i], refs[n + i], refs[2 * n].at[i]) for i in range(n)
        ]
        for c in copies:
            c.start()
        for c in copies:
            c.wait()

    moved = sum(w.size * 2 for w in weights)
    return pl.pallas_call(
        kernel,
        in_specs=[pl.BlockSpec(memory_space=pltpu.HBM)] * n,
        out_specs=[VM] * n,
        out_shape=[pltpu.VMEM(w.shape, w.dtype) for w in weights],
        scratch_shapes=[pltpu.SemaphoreType.DMA((n,))],
        compiler_params=pltpu.CompilerParams(vmem_limit_bytes=1 << 20),
        cost_estimate=pl.CostEstimate(flops=0, bytes_accessed=2 * moved, transcendentals=0),
    )(*weights)


def gate_up(idx, chunks, weights, narrow):
    tokens, width = chunks[0].shape
    feats = 8 * width
    units = weights[0].shape[-1]
    block = 256
    rows = tokens // 4
    mid_rows = tokens // 8
    n_w = len(weights)

    def kernel(idx_ref, *refs):
        xs, ws = refs[:8], refs[8 : 8 + n_w]
        outs = refs[8 + n_w : 12 + n_w]
        mid, lhs, val = refs[12 + n_w :]
        s, t, mix = idx_ref[0], idx_ref[1], idx_ref[2]
        fill_features(lhs, xs, t, mix, narrow_slot if narrow else plain_slot)
        if narrow:
            row = pl.multiple_of(t * mid_rows, mid_rows)
            for k, ref in enumerate(xs):
                owner = lax.rem(t - k + 8, 8)
                to = pl.multiple_of(owner * width, width)
                mid[:, pl.ds(to, width)] = ref[pl.ds(row, mid_rows), :]
        for g in range(2):
            for at in range(0, units, block):
                size = min(block, units - at)
                if narrow:
                    value = None
                    for j, w in enumerate(ws):
                        term = jnp.dot(
                            lhs[:, j * width : (j + 1) * width],
                            w[g, :, at : at + size],
                            preferred_element_type=F32,
                        )
                        value = term if value is None else value + term
                else:
                    value = jnp.dot(lhs[...], ws[g][:, at : at + size], preferred_element_type=F32)
                val[:, :size] = value
                for r, out in enumerate(outs):
                    row = pl.multiple_of(lax.rem(s + r, 4) * rows, rows)
                    out[g, :, at : at + size] = val[pl.ds(row, rows), :size].astype(out.dtype)

    res = call(
        kernel,
        idx,
        (*chunks, *weights),
        [((2, rows, units), F32)] + [((2, rows, units), BF)] * 3 + [((mid_rows, feats), BF)],
        [pltpu.VMEM((tokens, feats), BF), pltpu.VMEM((tokens, block), F32)],
        4 * tokens * feats * units,
        4 * feats * units,
    )
    return res[0], res[1:4], res[4]


def down_wide_part(idx, chunks, down_w):
    rows, units = chunks[0].shape
    tokens = 4 * rows
    feats = down_w.shape[1]
    width = feats // 8

    def kernel(idx_ref, *refs):
        hs, w, out, lhs = refs[:4], refs[4], refs[5], refs[6]
        fill_rows(lhs, hs, idx_ref[0], 4)
        for k in range(8):
            out[k] = jnp.dot(
                lhs[...], w[:, k * width : (k + 1) * width], preferred_element_type=F32
            ).astype(BF)

    return call(
        kernel,
        idx,
        (*chunks, down_w),
        [((8, tokens, width), BF)],
        [pltpu.VMEM((tokens, units), BF)],
        2 * tokens * feats * units,
        2 * feats * units,
    )[0]


def down_narrow_part(idx, chunks, weights):
    _, rows, units = chunks[0].shape
    tokens = 4 * rows
    width = weights[0].shape[1]
    feats = 8 * width

    def kernel(idx_ref, *refs):
        hs, ws, out, lhs = refs[:4], refs[4:12], refs[12], refs[13]
        mix = idx_ref[2]
        for k, h in enumerate(hs):
            row = pl.multiple_of(lax.rem(idx_ref[0] - k + 4, 4) * rows, rows)
            lhs[pl.ds(row, rows), :] = h[2]
        for j, w in enumerate(ws):
            at = pl.multiple_of(narrow_owner(j, mix) * width, width)
            out[:, pl.ds(at, width)] = lax.dot_general(
                lhs[...], w[2], NT, preferred_element_type=F32
            )

    return call(
        kernel,
        idx,
        (*chunks, *weights),
        [((tokens, feats), F32)],
        [pltpu.VMEM((tokens, units), BF)],
        2 * tokens * feats * units,
        2 * feats * units,
    )[0]


def hidden_grad_wide(idx, chunks, down_w):
    tokens, width = chunks[0].shape
    feats = 8 * width
    units = down_w.shape[0]
    block = 256
    rows = tokens // 4

    def kernel(idx_ref, *refs):
        xs, w, outs, lhs, val = refs[:8], refs[8], refs[9:13], refs[13], refs[14]
        s, t = idx_ref[0], idx_ref[1]
        fill_features(lhs, xs, t, 0, plain_slot)
        for at in range(0, units, block):
            val[...] = lax.dot_general(
                lhs[...], w[at : at + block, :], NT, preferred_element_type=F32
            )
            for r, out in enumerate(outs):
                row = pl.multiple_of(lax.rem(s + r, 4) * rows, rows)
                out[:, at : at + block] = val[pl.ds(row, rows), :].astype(out.dtype)

    res = call(
        kernel,
        idx,
        (*chunks, down_w),
        [((rows, units), F32)] + [((rows, units), BF)] * 3,
        [pltpu.VMEM((tokens, feats), BF), pltpu.VMEM((tokens, block), F32)],
        2 * tokens * feats * units,
        2 * feats * units,
    )
    return res[0], res[1:]


def hidden_grad_narrow(idx, cot, weights):
    tokens, feats = cot.shape
    width = feats // 8
    units = weights[0].shape[2]
    block = 256
    rows = tokens // 4

    def kernel(idx_ref, *refs):
        lhs, ws, outs = refs[0], refs[1:9], refs[9:13]
        own, val = refs[13:]
        s, t, mix = idx_ref[0], idx_ref[1], idx_ref[2]
        own[...] = lhs[:, pl.ds(pl.multiple_of(t * width, width), width)]
        for at in range(0, units, block):
            size = min(block, units - at)
            total = None
            for j, w in enumerate(ws):
                left = lhs[:, pl.ds(pl.multiple_of(narrow_owner(j, mix) * width, width), width)]
                term = jnp.dot(left, w[2, :, at : at + size], preferred_element_type=F32)
                total = term if total is None else total + term
            val[:, :size] = total
            for r, out in enumerate(outs):
                row = pl.multiple_of(lax.rem(s + r, 4) * rows, rows)
                out[:, at : at + size] = val[pl.ds(row, rows), :size].astype(out.dtype)

    res = call(
        kernel,
        idx,
        (cot, *weights),
        [((rows, units), F32)] + [((rows, units), BF)] * 3 + [((tokens, width), BF)],
        [pltpu.VMEM((tokens, block), F32)],
        2 * tokens * feats * units,
        2 * feats * units,
    )
    return res[0], res[1:4], res[4]


def input_back_wide(idx, chunks, gate_w, up_w):
    _, rows, units = chunks[0].shape
    tokens = 4 * rows
    width = gate_w.shape[0] // 8
    feats = 8 * width

    def kernel(idx_ref, *refs):
        ps, g, u, out, lhs = refs[:4], refs[4], refs[5], refs[6], refs[7]
        fill_rows(lhs, ps, idx_ref[0], 4)
        for k in range(8):
            rows_k = slice(k * width, (k + 1) * width)
            value = lax.dot_general(lhs[0], g[rows_k, :], NT, preferred_element_type=F32)
            value += lax.dot_general(lhs[1], u[rows_k, :], NT, preferred_element_type=F32)
            out[k] = value.astype(BF)

    return call(
        kernel,
        idx,
        (*chunks, gate_w, up_w),
        [((8, tokens, width), BF)],
        [pltpu.VMEM((2, tokens, units), BF)],
        4 * tokens * feats * units,
        4 * feats * units,
    )[0]


def input_back_narrow(idx, chunks, weights):
    _, rows, units = chunks[0].shape
    tokens = 4 * rows
    width = weights[0].shape[1]
    feats = 8 * width

    def kernel(idx_ref, *refs):
        ps, ws, out, lhs = refs[:4], refs[4:12], refs[12], refs[13]
        mix = idx_ref[2]
        fill_rows(lhs, ps, idx_ref[0], 4)
        for j, w in enumerate(ws):
            value = lax.dot_general(lhs[0], w[0], NT, preferred_element_type=F32)
            value += lax.dot_general(lhs[1], w[1], NT, preferred_element_type=F32)
            out[narrow_owner(j, mix)] = value.astype(BF)

    return call(
        kernel,
        idx,
        (*chunks, *weights),
        [((8, tokens, width), BF)],
        [pltpu.VMEM((2, tokens, units), BF)],
        4 * tokens * feats * units,
        4 * feats * units,
    )[0]


def add_up(own, received):
    total = own
    for r in received:
        total = total + r.astype(F32)
    return total


def add_over_tensor(base, parts):
    received = lax.all_to_all(parts, "tensor", split_axis=0, concat_axis=0, tiled=True)
    return (base.astype(F32) + jnp.sum(received.astype(F32), axis=0)).astype(BF)


def hidden_of(gate, upper, mask):
    sigma = jax.nn.sigmoid(gate)
    return (gate * sigma * upper * mask).astype(BF)


def grads_of(dhid, gate, upper, mask):
    sigma = jax.nn.sigmoid(gate)
    dgate = (dhid * upper * sigma * (1.0 + gate * (1.0 - sigma)) * mask).astype(BF)
    dup = (dhid * gate * sigma * mask).astype(BF)
    return [dgate, dup]


def after(value, *earlier):
    return lax.optimization_barrier((value, earlier))[0]


CORES = [(0, 1), (1, 0), (2, 3), (3, 2)]


def own_half(w, tensor, flip):
    size = w.shape[2] // 2
    return lax.dynamic_slice_in_dim(w, (((tensor >> 1) & 1) ^ flip) * size, size, 2)


def hand_out(piece, flip_x, flip_half):
    perm = []
    for d in range(4):
        for t in range(8):
            g, a, b = t >> 2, (t >> 1) & 1, t & 1
            to_d = (g ^ flip_x) * 2 + b
            to_t = 4 * (d & 1) + 2 * (d >> 1) + (a ^ flip_half)
            perm.append((d * 8 + t, to_d * 8 + to_t))
    return lax.ppermute(piece, ("dp", "tensor"), perm)


def to_sibling(pieces):
    return [lax.ppermute(p, "dp", CORES) for p in pieces]


def body(
    inputs,
    gate_wide,
    up_wide,
    down_wide,
    width_wide,
    gate_narrow,
    up_narrow,
    down_narrow,
    width_narrow,
    cotangent,
):
    section = lax.axis_index("section").astype(jnp.int32)
    tensor = lax.axis_index("tensor").astype(jnp.int32)
    dp = lax.axis_index("dp").astype(jnp.int32)
    mix = (dp & 1) * 4 + (dp >> 1) * 2 + (tensor & 1)
    idx = jnp.stack([section, tensor, mix])
    units_a = gate_wide.shape[1]
    units_b = gate_narrow.shape[1] // 2
    mask_a = (
        tensor * units_a + jnp.arange(units_a, dtype=jnp.int32) < width_wide[0]
    ).astype(F32)
    from_dp = 2 * ((tensor >> 1) & 1) + (tensor >> 2)
    mask_b = (
        (2 * from_dp + (tensor & 1)) * units_b + jnp.arange(units_b, dtype=jnp.int32) < width_narrow[0]
    ).astype(F32)
    blocks, quarter, width = inputs.shape
    tokens = blocks * quarter
    own_in = inputs.reshape(tokens, width)

    narrow = jnp.stack([gate_narrow, up_narrow, down_narrow.T])
    half = [own_half(narrow, tensor, j) for j in range(2)]
    cot_rows = lax.all_gather(cotangent[0], "tensor", axis=0, tiled=True)
    x_chunks = spread(own_in, "tensor", 8)
    gate_1, up_1 = into_vmem(*after((gate_wide, up_wide), x_chunks[1], x_chunks[2]))
    ready = after(half, x_chunks)
    a00, a11 = hand_out(ready[0], 0, 0), hand_out(ready[1], 1, 1)
    ready = after(half, (a00, a11))
    a01, a10 = hand_out(ready[1], 0, 1), hand_out(ready[0], 1, 0)

    own, parts, _ = gate_up(idx, x_chunks, (gate_1, up_1), False)
    down_1, = into_vmem(after(down_wide, own))
    both_a = add_up(own, send(parts, "section", 4))
    hidden_a = after(hidden_of(both_a[0], both_a[1], mask_a), (a00, a11))
    hidden_chunks = after(spread(hidden_a, "section", 4), down_1)
    s00, s11 = to_sibling(after([a00, a11], hidden_chunks))
    parts = after(down_wide_part(idx, hidden_chunks, down_1), (a01, a10))
    middle = add_over_tensor(own_in, parts)
    middle = after(middle, cot_rows)
    s01, s10 = to_sibling(after([a01, a10], middle))
    pieces = [a00, a01, a10, a11, s00, s01, s10, s11]
    mid_chunks = spread(middle, "tensor", 8)
    own, parts, cot_own = hidden_grad_narrow(idx, cot_rows, pieces)
    dhid_b = add_up(own, send(parts, "section", 4))
    mid_chunks = after(mid_chunks, cot_own)
    own, parts, mid_rows = gate_up(idx, mid_chunks, pieces, True)
    both_b = add_up(own, send(parts, "section", 4))

    hidden_b = hidden_of(both_b[0], both_b[1], mask_b)
    three_b = jnp.stack(grads_of(dhid_b, both_b[0], both_b[1], mask_b) + [hidden_b])
    three_chunks = spread(three_b, "section", 4)
    parts = input_back_narrow(idx, three_chunks, pieces)
    out_part = down_narrow_part(idx, after(three_chunks, parts), pieces)
    middle_grad = after(add_over_tensor(cot_own, parts), out_part)
    grad_chunks = spread(middle_grad, "tensor", 8)
    down_2, = into_vmem(after(down_wide, middle_grad))
    grad_chunks = after(grad_chunks, down_2)
    own, parts = hidden_grad_wide(idx, grad_chunks, down_2)

    received = send(parts, "section", 4)
    out_sum = lax.psum_scatter(after(out_part, own), "tensor", scatter_dimension=0, tiled=True)
    outputs = (mid_rows.astype(F32) + out_sum).astype(BF)

    gate_2, = into_vmem(after(gate_wide, own))
    dhid_a = add_up(own, after(received, gate_2))
    pair_a = jnp.stack(grads_of(dhid_a, both_a[0], both_a[1], mask_a))
    up_2, = into_vmem(after(up_wide, dhid_a))
    pair_chunks = after(spread(pair_a, "section", 4), up_2)
    input_grad = add_over_tensor(middle_grad, input_back_wide(idx, pair_chunks, gate_2, up_2))
    return (
        outputs.reshape(1, quarter, outputs.shape[1]),
        input_grad.reshape(blocks, quarter, width),
    )


def solution(mesh):
    in_specs = (
        P(None, "dp", ("section", "tensor")),
        P("section", "tensor"),
        P("section", "tensor"),
        P("tensor", "section"),
        P(),
        P(("section", "tensor"), "dp"),
        P(("section", "tensor"), "dp"),
        P("dp", ("section", "tensor")),
        P(),
        P("tensor", "dp", "section"),
    )
    out_specs = (P("tensor", "dp", "section"), P(None, "dp", ("section", "tensor")))
    return jax.shard_map(body, mesh=mesh, in_specs=in_specs, out_specs=out_specs, check_vma=False)
```

```python
import jax
import jax.numpy as jnp
from jax import lax
from jax.experimental import pallas as pl
from jax.experimental.pallas import tpu as pltpu
from jax.sharding import PartitionSpec as P

BF = jnp.bfloat16
F32 = jnp.float32
VMEM = 8 << 20
NT = (((1,), (1,)), ((), ()))


def ring(n, shift):
    return [(i, (i + shift) % n) for i in range(n)]


def send(parts, axis, n):
    return [lax.ppermute(p, axis, ring(n, r)) for r, p in zip(range(1, n), parts)]


def spread(own, axis, n):
    return [own] + send([own] * (n - 1), axis, n)


VM = pl.BlockSpec(memory_space=pltpu.VMEM)
SM = pl.BlockSpec(memory_space=pltpu.SMEM)


def fill_features(scratch, refs, t, mix, slot):
    width = refs[0].shape[1]
    for k, ref in enumerate(refs):
        owner = lax.rem(t - k + 8, 8)
        at = pl.multiple_of(slot(owner, mix) * width, width)
        scratch[:, pl.ds(at, width)] = ref[...]


def fill_rows(scratch, refs, me, n):
    rows = refs[0].shape[-2]
    for k, ref in enumerate(refs):
        at = pl.multiple_of(lax.rem(me - k + n, n) * rows, rows)
        if len(ref.shape) == 3:
            for g in range(2):
                scratch[g, pl.ds(at, rows), :] = ref[g]
        else:
            scratch[pl.ds(at, rows), :] = ref[...]


def plain_slot(owner, mix):
    return owner


def narrow_slot(owner, mix):
    return (((owner & 1) << 2) | (owner >> 1)) ^ mix


def narrow_owner(slot, mix):
    swapped = slot ^ mix
    return ((swapped & 3) << 1) | (swapped >> 2)


def call(kernel, idx, operands, outs, scratch, flops, moved):
    return pl.pallas_call(
        kernel,
        in_specs=[SM] + [VM] * len(operands),
        out_specs=[VM] * len(outs),
        out_shape=[pltpu.VMEM(shape, kind) for shape, kind in outs],
        scratch_shapes=scratch,
        compiler_params=pltpu.CompilerParams(vmem_limit_bytes=VMEM),
        cost_estimate=pl.CostEstimate(flops=flops, bytes_accessed=moved, transcendentals=0),
    )(idx, *operands)


def into_vmem(*weights):
    n = len(weights)

    def kernel(*refs):
        copies = [
            pltpu.make_async_copy(refs[i], refs[n + i], refs[2 * n].at[i]) for i in range(n)
        ]
        for c in copies:
            c.start()
        for c in copies:
            c.wait()

    moved = sum(w.size * 2 for w in weights)
    return pl.pallas_call(
        kernel,
        in_specs=[pl.BlockSpec(memory_space=pltpu.HBM)] * n,
        out_specs=[VM] * n,
        out_shape=[pltpu.VMEM(w.shape, w.dtype) for w in weights],
        scratch_shapes=[pltpu.SemaphoreType.DMA((n,))],
        compiler_params=pltpu.CompilerParams(vmem_limit_bytes=1 << 20),
        cost_estimate=pl.CostEstimate(flops=0, bytes_accessed=2 * moved, transcendentals=0),
    )(*weights)


def gate_up(idx, chunks, weights, narrow):
    tokens, width = chunks[0].shape
    feats = 8 * width
    units = weights[0].shape[-1]
    block = 256
    rows = tokens // 4
    mid_rows = tokens // 8
    n_w = len(weights)

    def kernel(idx_ref, *refs):
        xs, ws = refs[:8], refs[8 : 8 + n_w]
        outs = refs[8 + n_w : 12 + n_w]
        mid, lhs, val = refs[12 + n_w :]
        s, t, mix = idx_ref[0], idx_ref[1], idx_ref[2]
        fill_features(lhs, xs, t, mix, narrow_slot if narrow else plain_slot)
        if narrow:
            row = pl.multiple_of(t * mid_rows, mid_rows)
            for k, ref in enumerate(xs):
                owner = lax.rem(t - k + 8, 8)
                to = pl.multiple_of(owner * width, width)
                mid[:, pl.ds(to, width)] = ref[pl.ds(row, mid_rows), :]
        for g in range(2):
            for at in range(0, units, block):
                size = min(block, units - at)
                if narrow:
                    value = None
                    for j, w in enumerate(ws):
                        term = jnp.dot(
                            lhs[:, j * width : (j + 1) * width],
                            w[g, :, at : at + size],
                            preferred_element_type=F32,
                        )
                        value = term if value is None else value + term
                else:
                    value = jnp.dot(lhs[...], ws[g][:, at : at + size], preferred_element_type=F32)
                val[:, :size] = value
                for r, out in enumerate(outs):
                    row = pl.multiple_of(lax.rem(s + r, 4) * rows, rows)
                    out[g, :, at : at + size] = val[pl.ds(row, rows), :size].astype(out.dtype)

    res = call(
        kernel,
        idx,
        (*chunks, *weights),
        [((2, rows, units), F32)] + [((2, rows, units), BF)] * 3 + [((mid_rows, feats), BF)],
        [pltpu.VMEM((tokens, feats), BF), pltpu.VMEM((tokens, block), F32)],
        4 * tokens * feats * units,
        4 * feats * units,
    )
    return res[0], res[1:4], res[4]


def down_wide_part(idx, chunks, down_w):
    rows, units = chunks[0].shape
    tokens = 4 * rows
    feats = down_w.shape[1]
    width = feats // 8

    def kernel(idx_ref, *refs):
        hs, w, out, lhs = refs[:4], refs[4], refs[5], refs[6]
        fill_rows(lhs, hs, idx_ref[0], 4)
        for k in range(8):
            out[k] = jnp.dot(
                lhs[...], w[:, k * width : (k + 1) * width], preferred_element_type=F32
            ).astype(BF)

    return call(
        kernel,
        idx,
        (*chunks, down_w),
        [((8, tokens, width), BF)],
        [pltpu.VMEM((tokens, units), BF)],
        2 * tokens * feats * units,
        2 * feats * units,
    )[0]


def down_narrow_part(idx, chunks, weights):
    _, rows, units = chunks[0].shape
    tokens = 4 * rows
    width = weights[0].shape[1]
    feats = 8 * width

    def kernel(idx_ref, *refs):
        hs, ws, out, lhs = refs[:4], refs[4:12], refs[12], refs[13]
        mix = idx_ref[2]
        for k, h in enumerate(hs):
            row = pl.multiple_of(lax.rem(idx_ref[0] - k + 4, 4) * rows, rows)
            lhs[pl.ds(row, rows), :] = h[2]
        for j, w in enumerate(ws):
            at = pl.multiple_of(narrow_owner(j, mix) * width, width)
            out[:, pl.ds(at, width)] = lax.dot_general(
                lhs[...], w[2], NT, preferred_element_type=F32
            ).astype(BF)

    return call(
        kernel,
        idx,
        (*chunks, *weights),
        [((tokens, feats), BF)],
        [pltpu.VMEM((tokens, units), BF)],
        2 * tokens * feats * units,
        2 * feats * units,
    )[0]


def hidden_grad_wide(idx, chunks, down_w):
    tokens, width = chunks[0].shape
    feats = 8 * width
    units = down_w.shape[0]
    block = 256
    rows = tokens // 4

    def kernel(idx_ref, *refs):
        xs, w, outs, lhs, val = refs[:8], refs[8], refs[9:13], refs[13], refs[14]
        s, t = idx_ref[0], idx_ref[1]
        fill_features(lhs, xs, t, 0, plain_slot)
        for at in range(0, units, block):
            val[...] = lax.dot_general(
                lhs[...], w[at : at + block, :], NT, preferred_element_type=F32
            )
            for r, out in enumerate(outs):
                row = pl.multiple_of(lax.rem(s + r, 4) * rows, rows)
                out[:, at : at + block] = val[pl.ds(row, rows), :].astype(out.dtype)

    res = call(
        kernel,
        idx,
        (*chunks, down_w),
        [((rows, units), F32)] + [((rows, units), BF)] * 3,
        [pltpu.VMEM((tokens, feats), BF), pltpu.VMEM((tokens, block), F32)],
        2 * tokens * feats * units,
        2 * feats * units,
    )
    return res[0], res[1:]


def hidden_grad_narrow(idx, cot, weights):
    tokens, feats = cot.shape
    width = feats // 8
    units = weights[0].shape[2]
    block = 256
    rows = tokens // 4

    def kernel(idx_ref, *refs):
        lhs, ws, outs = refs[0], refs[1:9], refs[9:13]
        own, val = refs[13:]
        s, t, mix = idx_ref[0], idx_ref[1], idx_ref[2]
        own[...] = lhs[:, pl.ds(pl.multiple_of(t * width, width), width)]
        for at in range(0, units, block):
            size = min(block, units - at)
            total = None
            for j, w in enumerate(ws):
                left = lhs[:, pl.ds(pl.multiple_of(narrow_owner(j, mix) * width, width), width)]
                term = jnp.dot(left, w[2, :, at : at + size], preferred_element_type=F32)
                total = term if total is None else total + term
            val[:, :size] = total
            for r, out in enumerate(outs):
                row = pl.multiple_of(lax.rem(s + r, 4) * rows, rows)
                out[:, at : at + size] = val[pl.ds(row, rows), :size].astype(out.dtype)

    res = call(
        kernel,
        idx,
        (cot, *weights),
        [((rows, units), F32)] + [((rows, units), BF)] * 3 + [((tokens, width), BF)],
        [pltpu.VMEM((tokens, block), F32)],
        2 * tokens * feats * units,
        2 * feats * units,
    )
    return res[0], res[1:4], res[4]


def input_back_wide(idx, chunks, gate_w, up_w):
    _, rows, units = chunks[0].shape
    tokens = 4 * rows
    width = gate_w.shape[0] // 8
    feats = 8 * width

    def kernel(idx_ref, *refs):
        ps, g, u, out, lhs = refs[:4], refs[4], refs[5], refs[6], refs[7]
        fill_rows(lhs, ps, idx_ref[0], 4)
        for k in range(8):
            rows_k = slice(k * width, (k + 1) * width)
            value = lax.dot_general(lhs[0], g[rows_k, :], NT, preferred_element_type=F32)
            value += lax.dot_general(lhs[1], u[rows_k, :], NT, preferred_element_type=F32)
            out[k] = value.astype(BF)

    return call(
        kernel,
        idx,
        (*chunks, gate_w, up_w),
        [((8, tokens, width), BF)],
        [pltpu.VMEM((2, tokens, units), BF)],
        4 * tokens * feats * units,
        4 * feats * units,
    )[0]


def input_back_narrow(idx, chunks, weights):
    _, rows, units = chunks[0].shape
    tokens = 4 * rows
    width = weights[0].shape[1]
    feats = 8 * width

    def kernel(idx_ref, *refs):
        ps, ws, out, lhs = refs[:4], refs[4:12], refs[12], refs[13]
        mix = idx_ref[2]
        fill_rows(lhs, ps, idx_ref[0], 4)
        for j, w in enumerate(ws):
            value = lax.dot_general(lhs[0], w[0], NT, preferred_element_type=F32)
            value += lax.dot_general(lhs[1], w[1], NT, preferred_element_type=F32)
            out[narrow_owner(j, mix)] = value.astype(BF)

    return call(
        kernel,
        idx,
        (*chunks, *weights),
        [((8, tokens, width), BF)],
        [pltpu.VMEM((2, tokens, units), BF)],
        4 * tokens * feats * units,
        4 * feats * units,
    )[0]


def add_up(own, received):
    total = own
    for r in received:
        total = total + r.astype(F32)
    return total


def add_over_tensor(base, parts):
    received = lax.all_to_all(parts, "tensor", split_axis=0, concat_axis=0, tiled=True)
    return (base.astype(F32) + jnp.sum(received.astype(F32), axis=0)).astype(BF)


def hidden_of(gate, upper, mask):
    sigma = jax.nn.sigmoid(gate)
    return (gate * sigma * upper * mask).astype(BF)


def grads_of(dhid, gate, upper, mask):
    sigma = jax.nn.sigmoid(gate)
    dgate = (dhid * upper * sigma * (1.0 + gate * (1.0 - sigma)) * mask).astype(BF)
    dup = (dhid * gate * sigma * mask).astype(BF)
    return [dgate, dup]


def after(value, *earlier):
    return lax.optimization_barrier((value, earlier))[0]


CORES = [(0, 1), (1, 0), (2, 3), (3, 2)]


def own_halves(idx, gate_w, up_w, down_w):
    width, units = gate_w.shape
    size = units // 2

    def kernel(idx_ref, g, u, d, *outs):
        bit = (idx_ref[1] >> 1) & 1
        for j, out in enumerate(outs):
            at = pl.multiple_of((bit ^ j) * size, size)
            out[0] = g[:, pl.ds(at, size)]
            out[1] = u[:, pl.ds(at, size)]
            out[2] = d[pl.ds(at, size), :].T

    return call(
        kernel,
        idx,
        (gate_w, up_w, down_w),
        [((3, width, size), BF)] * 2,
        [],
        0,
        12 * width * units,
    )


def hand_out(piece, flip_x, flip_half):
    perm = []
    for d in range(4):
        for t in range(8):
            g, a, b = t >> 2, (t >> 1) & 1, t & 1
            to_d = (g ^ flip_x) * 2 + b
            to_t = 4 * (d & 1) + 2 * (d >> 1) + (a ^ flip_half)
            perm.append((d * 8 + t, to_d * 8 + to_t))
    return lax.ppermute(piece, ("dp", "tensor"), perm)


def to_sibling(pieces):
    return [lax.ppermute(p, "dp", CORES) for p in pieces]


def body(
    inputs,
    gate_wide,
    up_wide,
    down_wide,
    width_wide,
    gate_narrow,
    up_narrow,
    down_narrow,
    width_narrow,
    cotangent,
):
    section = lax.axis_index("section").astype(jnp.int32)
    tensor = lax.axis_index("tensor").astype(jnp.int32)
    dp = lax.axis_index("dp").astype(jnp.int32)
    mix = (dp & 1) * 4 + (dp >> 1) * 2 + (tensor & 1)
    idx = jnp.stack([section, tensor, mix])
    units_a = gate_wide.shape[1]
    units_b = gate_narrow.shape[1] // 2
    mask_a = (
        tensor * units_a + jnp.arange(units_a, dtype=jnp.int32) < width_wide[0]
    ).astype(F32)
    from_dp = 2 * ((tensor >> 1) & 1) + (tensor >> 2)
    mask_b = (
        (2 * from_dp + (tensor & 1)) * units_b + jnp.arange(units_b, dtype=jnp.int32) < width_narrow[0]
    ).astype(F32)
    blocks, quarter, width = inputs.shape
    tokens = blocks * quarter
    own_in = inputs.reshape(tokens, width)

    half = own_halves(idx, gate_narrow, up_narrow, down_narrow)
    cot_rows = lax.all_gather(cotangent[0], "tensor", axis=0, tiled=True)
    x_chunks = spread(own_in, "tensor", 8)
    gate_1, up_1 = into_vmem(*after((gate_wide, up_wide), x_chunks[1], x_chunks[2]))
    x_chunks = after(x_chunks, half)
    ready = after(half, x_chunks)
    a00, a11 = hand_out(ready[0], 0, 0), hand_out(ready[1], 1, 1)
    ready = after(half, (a00, a11))
    a01, a10 = hand_out(ready[1], 0, 1), hand_out(ready[0], 1, 0)

    own, parts, _ = gate_up(idx, x_chunks, (gate_1, up_1), False)
    down_1, = into_vmem(after(down_wide, own))
    both_a = add_up(own, send(parts, "section", 4))
    hidden_a = after(hidden_of(both_a[0], both_a[1], mask_a), (a00, a11))
    hidden_chunks = after(spread(hidden_a, "section", 4), down_1)
    s00, s11 = to_sibling(after([a00, a11], hidden_chunks))
    parts = after(down_wide_part(idx, hidden_chunks, down_1), (a01, a10))
    middle = add_over_tensor(own_in, parts)
    middle = after(middle, cot_rows)
    s01, s10 = to_sibling(after([a01, a10], middle))
    pieces = [a00, a01, a10, a11, s00, s01, s10, s11]
    mid_chunks = spread(middle, "tensor", 8)
    own, parts, cot_own = hidden_grad_narrow(idx, cot_rows, pieces)
    dhid_b = add_up(own, send(parts, "section", 4))
    mid_chunks = after(mid_chunks, cot_own)
    own, parts, mid_rows = gate_up(idx, mid_chunks, pieces, True)
    both_b = add_up(own, send(parts, "section", 4))

    hidden_b = hidden_of(both_b[0], both_b[1], mask_b)
    three_b = jnp.stack(grads_of(dhid_b, both_b[0], both_b[1], mask_b) + [hidden_b])
    three_chunks = spread(three_b, "section", 4)
    parts = input_back_narrow(idx, three_chunks, pieces)
    out_part = down_narrow_part(idx, after(three_chunks, parts), pieces)
    middle_grad = after(add_over_tensor(cot_own, parts), out_part)
    grad_chunks = spread(middle_grad, "tensor", 8)
    down_2, = into_vmem(after(down_wide, middle_grad))
    grad_chunks = after(grad_chunks, down_2)
    own, parts = hidden_grad_wide(idx, grad_chunks, down_2)

    received = send(parts, "section", 4)
    out_sum = lax.psum_scatter(after(out_part, own), "tensor", scatter_dimension=0, tiled=True)
    outputs = (mid_rows.astype(F32) + out_sum.astype(F32)).astype(BF)

    gate_2, = into_vmem(after(gate_wide, own))
    dhid_a = add_up(own, after(received, gate_2))
    pair_a = jnp.stack(grads_of(dhid_a, both_a[0], both_a[1], mask_a))
    up_2, = into_vmem(after(up_wide, dhid_a))
    pair_chunks = after(spread(pair_a, "section", 4), up_2)
    input_grad = add_over_tensor(middle_grad, input_back_wide(idx, pair_chunks, gate_2, up_2))
    return (
        outputs.reshape(1, quarter, outputs.shape[1]),
        input_grad.reshape(blocks, quarter, width),
    )


def solution(mesh):
    in_specs = (
        P(None, "dp", ("section", "tensor")),
        P("section", "tensor"),
        P("section", "tensor"),
        P("tensor", "section"),
        P(),
        P(("section", "tensor"), "dp"),
        P(("section", "tensor"), "dp"),
        P("dp", ("section", "tensor")),
        P(),
        P("tensor", "dp", "section"),
    )
    out_specs = (P("tensor", "dp", "section"), P(None, "dp", ("section", "tensor")))
    return jax.shard_map(body, mesh=mesh, in_specs=in_specs, out_specs=out_specs, check_vma=False)
```

```python
import jax
import jax.numpy as jnp
from jax import lax
from jax.experimental import pallas as pl
from jax.experimental.pallas import tpu as pltpu
from jax.sharding import PartitionSpec as P

BF = jnp.bfloat16
F32 = jnp.float32
VMEM = 8 << 20
NT = (((1,), (1,)), ((), ()))


def ring(n, shift):
    return [(i, (i + shift) % n) for i in range(n)]


def send(parts, axis, n):
    return [lax.ppermute(p, axis, ring(n, r)) for r, p in zip(range(1, n), parts)]


def spread(own, axis, n):
    return [own] + send([own] * (n - 1), axis, n)


VM = pl.BlockSpec(memory_space=pltpu.VMEM)
SM = pl.BlockSpec(memory_space=pltpu.SMEM)


def fill_features(scratch, refs, t, mix, slot):
    width = refs[0].shape[1]
    for k, ref in enumerate(refs):
        owner = lax.rem(t - k + 8, 8)
        at = pl.multiple_of(slot(owner, mix) * width, width)
        scratch[:, pl.ds(at, width)] = ref[...]


def fill_rows(scratch, refs, me, n):
    rows = refs[0].shape[-2]
    for k, ref in enumerate(refs):
        at = pl.multiple_of(lax.rem(me - k + n, n) * rows, rows)
        if len(ref.shape) == 3:
            for g in range(2):
                scratch[g, pl.ds(at, rows), :] = ref[g]
        else:
            scratch[pl.ds(at, rows), :] = ref[...]


def plain_slot(owner, mix):
    return owner


def narrow_slot(owner, mix):
    return (((owner & 1) << 2) | (owner >> 1)) ^ mix


def narrow_owner(slot, mix):
    swapped = slot ^ mix
    return ((swapped & 3) << 1) | (swapped >> 2)


def call(kernel, idx, operands, outs, scratch, flops, moved):
    return pl.pallas_call(
        kernel,
        in_specs=[SM] + [VM] * len(operands),
        out_specs=[VM] * len(outs),
        out_shape=[pltpu.VMEM(shape, kind) for shape, kind in outs],
        scratch_shapes=scratch,
        compiler_params=pltpu.CompilerParams(vmem_limit_bytes=VMEM),
        cost_estimate=pl.CostEstimate(flops=flops, bytes_accessed=moved, transcendentals=0),
    )(idx, *operands)


def into_vmem(*weights):
    n = len(weights)

    def kernel(*refs):
        copies = [
            pltpu.make_async_copy(refs[i], refs[n + i], refs[2 * n].at[i]) for i in range(n)
        ]
        for c in copies:
            c.start()
        for c in copies:
            c.wait()

    moved = sum(w.size * 2 for w in weights)
    return pl.pallas_call(
        kernel,
        in_specs=[pl.BlockSpec(memory_space=pltpu.HBM)] * n,
        out_specs=[VM] * n,
        out_shape=[pltpu.VMEM(w.shape, w.dtype) for w in weights],
        scratch_shapes=[pltpu.SemaphoreType.DMA((n,))],
        compiler_params=pltpu.CompilerParams(vmem_limit_bytes=1 << 20),
        cost_estimate=pl.CostEstimate(flops=0, bytes_accessed=2 * moved, transcendentals=0),
    )(*weights)


def gate_up(idx, chunks, weights, narrow):
    tokens, width = chunks[0].shape
    feats = 8 * width
    units = weights[0].shape[-1]
    block = 256
    rows = tokens // 4
    mid_rows = tokens // 8
    n_w = len(weights)

    def kernel(idx_ref, *refs):
        xs, ws = refs[:8], refs[8 : 8 + n_w]
        outs = refs[8 + n_w : 12 + n_w]
        mid, lhs, val = refs[12 + n_w :]
        s, t, mix = idx_ref[0], idx_ref[1], idx_ref[2]
        fill_features(lhs, xs, t, mix, narrow_slot if narrow else plain_slot)
        if narrow:
            row = pl.multiple_of(t * mid_rows, mid_rows)
            for k, ref in enumerate(xs):
                owner = lax.rem(t - k + 8, 8)
                to = pl.multiple_of(owner * width, width)
                mid[:, pl.ds(to, width)] = ref[pl.ds(row, mid_rows), :]
        for g in range(2):
            for at in range(0, units, block):
                size = min(block, units - at)
                if narrow:
                    value = None
                    for j, w in enumerate(ws):
                        term = jnp.dot(
                            lhs[:, j * width : (j + 1) * width],
                            w[g, :, at : at + size],
                            preferred_element_type=F32,
                        )
                        value = term if value is None else value + term
                else:
                    value = jnp.dot(lhs[...], ws[g][:, at : at + size], preferred_element_type=F32)
                val[:, :size] = value
                for r, out in enumerate(outs):
                    row = pl.multiple_of(lax.rem(s + r, 4) * rows, rows)
                    out[g, :, at : at + size] = val[pl.ds(row, rows), :size].astype(out.dtype)

    res = call(
        kernel,
        idx,
        (*chunks, *weights),
        [((2, rows, units), F32)] + [((2, rows, units), BF)] * 3 + [((mid_rows, feats), BF)],
        [pltpu.VMEM((tokens, feats), BF), pltpu.VMEM((tokens, block), F32)],
        4 * tokens * feats * units,
        4 * feats * units,
    )
    return res[0], res[1:4], res[4]


def down_wide_part(idx, chunks, down_w):
    rows, units = chunks[0].shape
    tokens = 4 * rows
    feats = down_w.shape[1]
    width = feats // 8

    def kernel(idx_ref, *refs):
        hs, w, out, lhs = refs[:4], refs[4], refs[5], refs[6]
        fill_rows(lhs, hs, idx_ref[0], 4)
        for k in range(8):
            out[k] = jnp.dot(
                lhs[...], w[:, k * width : (k + 1) * width], preferred_element_type=F32
            ).astype(BF)

    return call(
        kernel,
        idx,
        (*chunks, down_w),
        [((8, tokens, width), BF)],
        [pltpu.VMEM((tokens, units), BF)],
        2 * tokens * feats * units,
        2 * feats * units,
    )[0]


def down_narrow_part(idx, chunks, weights):
    _, rows, units = chunks[0].shape
    tokens = 4 * rows
    width = weights[0].shape[1]
    feats = 8 * width

    def kernel(idx_ref, *refs):
        hs, ws, out, lhs = refs[:4], refs[4:12], refs[12], refs[13]
        mix = idx_ref[2]
        for k, h in enumerate(hs):
            row = pl.multiple_of(lax.rem(idx_ref[0] - k + 4, 4) * rows, rows)
            lhs[pl.ds(row, rows), :] = h[2]
        for j, w in enumerate(ws):
            at = pl.multiple_of(narrow_owner(j, mix) * width, width)
            out[:, pl.ds(at, width)] = lax.dot_general(
                lhs[...], w[2], NT, preferred_element_type=F32
            )

    return call(
        kernel,
        idx,
        (*chunks, *weights),
        [((tokens, feats), F32)],
        [pltpu.VMEM((tokens, units), BF)],
        2 * tokens * feats * units,
        2 * feats * units,
    )[0]


def hidden_grad_wide(idx, chunks, down_w):
    tokens, width = chunks[0].shape
    feats = 8 * width
    units = down_w.shape[0]
    block = 256
    rows = tokens // 4

    def kernel(idx_ref, *refs):
        xs, w, outs, lhs, val = refs[:8], refs[8], refs[9:13], refs[13], refs[14]
        s, t = idx_ref[0], idx_ref[1]
        fill_features(lhs, xs, t, 0, plain_slot)
        for at in range(0, units, block):
            val[...] = lax.dot_general(
                lhs[...], w[at : at + block, :], NT, preferred_element_type=F32
            )
            for r, out in enumerate(outs):
                row = pl.multiple_of(lax.rem(s + r, 4) * rows, rows)
                out[:, at : at + block] = val[pl.ds(row, rows), :].astype(out.dtype)

    res = call(
        kernel,
        idx,
        (*chunks, down_w),
        [((rows, units), F32)] + [((rows, units), BF)] * 3,
        [pltpu.VMEM((tokens, feats), BF), pltpu.VMEM((tokens, block), F32)],
        2 * tokens * feats * units,
        2 * feats * units,
    )
    return res[0], res[1:]


def hidden_grad_narrow(idx, cot, weights):
    tokens, feats = cot.shape
    width = feats // 8
    units = weights[0].shape[2]
    block = 256
    rows = tokens // 4

    def kernel(idx_ref, *refs):
        lhs, ws, outs = refs[0], refs[1:9], refs[9:13]
        own, val = refs[13:]
        s, t, mix = idx_ref[0], idx_ref[1], idx_ref[2]
        own[...] = lhs[:, pl.ds(pl.multiple_of(t * width, width), width)]
        for at in range(0, units, block):
            size = min(block, units - at)
            total = None
            for j, w in enumerate(ws):
                left = lhs[:, pl.ds(pl.multiple_of(narrow_owner(j, mix) * width, width), width)]
                term = jnp.dot(left, w[2, :, at : at + size], preferred_element_type=F32)
                total = term if total is None else total + term
            val[:, :size] = total
            for r, out in enumerate(outs):
                row = pl.multiple_of(lax.rem(s + r, 4) * rows, rows)
                out[:, at : at + size] = val[pl.ds(row, rows), :size].astype(out.dtype)

    res = call(
        kernel,
        idx,
        (cot, *weights),
        [((rows, units), F32)] + [((rows, units), BF)] * 3 + [((tokens, width), BF)],
        [pltpu.VMEM((tokens, block), F32)],
        2 * tokens * feats * units,
        2 * feats * units,
    )
    return res[0], res[1:4], res[4]


def input_back_wide(idx, chunks, gate_w, up_w):
    _, rows, units = chunks[0].shape
    tokens = 4 * rows
    width = gate_w.shape[0] // 8
    feats = 8 * width

    def kernel(idx_ref, *refs):
        ps, g, u, out, lhs = refs[:4], refs[4], refs[5], refs[6], refs[7]
        fill_rows(lhs, ps, idx_ref[0], 4)
        for k in range(8):
            rows_k = slice(k * width, (k + 1) * width)
            value = lax.dot_general(lhs[0], g[rows_k, :], NT, preferred_element_type=F32)
            value += lax.dot_general(lhs[1], u[rows_k, :], NT, preferred_element_type=F32)
            out[k] = value.astype(BF)

    return call(
        kernel,
        idx,
        (*chunks, gate_w, up_w),
        [((8, tokens, width), BF)],
        [pltpu.VMEM((2, tokens, units), BF)],
        4 * tokens * feats * units,
        4 * feats * units,
    )[0]


def input_back_narrow(idx, chunks, weights):
    _, rows, units = chunks[0].shape
    tokens = 4 * rows
    width = weights[0].shape[1]
    feats = 8 * width

    def kernel(idx_ref, *refs):
        ps, ws, out, lhs = refs[:4], refs[4:12], refs[12], refs[13]
        mix = idx_ref[2]
        fill_rows(lhs, ps, idx_ref[0], 4)
        for j, w in enumerate(ws):
            value = lax.dot_general(lhs[0], w[0], NT, preferred_element_type=F32)
            value += lax.dot_general(lhs[1], w[1], NT, preferred_element_type=F32)
            out[narrow_owner(j, mix)] = value.astype(BF)

    return call(
        kernel,
        idx,
        (*chunks, *weights),
        [((8, tokens, width), BF)],
        [pltpu.VMEM((2, tokens, units), BF)],
        4 * tokens * feats * units,
        4 * feats * units,
    )[0]


def add_up(own, received):
    total = own
    for r in received:
        total = total + r.astype(F32)
    return total


def add_over_tensor(base, parts):
    received = lax.all_to_all(parts, "tensor", split_axis=0, concat_axis=0, tiled=True)
    return (base.astype(F32) + jnp.sum(received.astype(F32), axis=0)).astype(BF)


def hidden_of(gate, upper, mask):
    sigma = jax.nn.sigmoid(gate)
    return (gate * sigma * upper * mask).astype(BF)


def grads_of(dhid, gate, upper, mask):
    sigma = jax.nn.sigmoid(gate)
    dgate = (dhid * upper * sigma * (1.0 + gate * (1.0 - sigma)) * mask).astype(BF)
    dup = (dhid * gate * sigma * mask).astype(BF)
    return [dgate, dup]


def after(value, *earlier):
    return lax.optimization_barrier((value, earlier))[0]


CORES = [(0, 1), (1, 0), (2, 3), (3, 2)]


def own_halves(idx, gate_w, up_w, down_w):
    width, units = gate_w.shape
    size = units // 2

    def kernel(idx_ref, g, u, d, *outs):
        bit = (idx_ref[1] >> 1) & 1
        for j, out in enumerate(outs):
            at = pl.multiple_of((bit ^ j) * size, size)
            out[0] = g[:, pl.ds(at, size)]
            out[1] = u[:, pl.ds(at, size)]
            out[2] = d[pl.ds(at, size), :].T

    return call(
        kernel,
        idx,
        (gate_w, up_w, down_w),
        [((3, width, size), BF)] * 2,
        [],
        0,
        12 * width * units,
    )


def hand_out(piece, flip_x, flip_half):
    perm = []
    for d in range(4):
        for t in range(8):
            g, a, b = t >> 2, (t >> 1) & 1, t & 1
            to_d = (g ^ flip_x) * 2 + b
            to_t = 4 * (d & 1) + 2 * (d >> 1) + (a ^ flip_half)
            perm.append((d * 8 + t, to_d * 8 + to_t))
    return lax.ppermute(piece, ("dp", "tensor"), perm)


def to_sibling(pieces):
    return [lax.ppermute(p, "dp", CORES) for p in pieces]


def body(
    inputs,
    gate_wide,
    up_wide,
    down_wide,
    width_wide,
    gate_narrow,
    up_narrow,
    down_narrow,
    width_narrow,
    cotangent,
):
    section = lax.axis_index("section").astype(jnp.int32)
    tensor = lax.axis_index("tensor").astype(jnp.int32)
    dp = lax.axis_index("dp").astype(jnp.int32)
    mix = (dp & 1) * 4 + (dp >> 1) * 2 + (tensor & 1)
    idx = jnp.stack([section, tensor, mix])
    units_a = gate_wide.shape[1]
    units_b = gate_narrow.shape[1] // 2
    mask_a = (
        tensor * units_a + jnp.arange(units_a, dtype=jnp.int32) < width_wide[0]
    ).astype(F32)
    from_dp = 2 * ((tensor >> 1) & 1) + (tensor >> 2)
    mask_b = (
        (2 * from_dp + (tensor & 1)) * units_b + jnp.arange(units_b, dtype=jnp.int32) < width_narrow[0]
    ).astype(F32)
    blocks, quarter, width = inputs.shape
    tokens = blocks * quarter
    own_in = inputs.reshape(tokens, width)

    half = own_halves(idx, gate_narrow, up_narrow, down_narrow)
    cot_rows = lax.all_gather(cotangent[0], "tensor", axis=0, tiled=True)
    x_chunks = spread(own_in, "tensor", 8)
    gate_1, up_1 = into_vmem(*after((gate_wide, up_wide), x_chunks[1], x_chunks[2]))
    x_chunks = after(x_chunks, half)
    ready = after(half, x_chunks)
    a00, a11 = hand_out(ready[0], 0, 0), hand_out(ready[1], 1, 1)
    ready = after(half, (a00, a11))
    a01, a10 = hand_out(ready[1], 0, 1), hand_out(ready[0], 1, 0)

    own, parts, _ = gate_up(idx, x_chunks, (gate_1, up_1), False)
    down_1, = into_vmem(after(down_wide, own))
    both_a = add_up(own, send(parts, "section", 4))
    hidden_a = after(hidden_of(both_a[0], both_a[1], mask_a), (a00, a11))
    hidden_chunks = after(spread(hidden_a, "section", 4), down_1)
    s00, s11 = to_sibling(after([a00, a11], hidden_chunks))
    parts = after(down_wide_part(idx, hidden_chunks, down_1), (a01, a10))
    middle = add_over_tensor(own_in, parts)
    middle = after(middle, cot_rows)
    s01, s10 = to_sibling(after([a01, a10], middle))
    pieces = [a00, a01, a10, a11, s00, s01, s10, s11]
    mid_chunks = spread(middle, "tensor", 8)
    own, parts, cot_own = hidden_grad_narrow(idx, cot_rows, pieces)
    dhid_b = add_up(own, send(parts, "section", 4))
    mid_chunks = after(mid_chunks, cot_own)
    own, parts, mid_rows = gate_up(idx, mid_chunks, pieces, True)
    both_b = add_up(own, send(parts, "section", 4))

    hidden_b = hidden_of(both_b[0], both_b[1], mask_b)
    three_b = jnp.stack(grads_of(dhid_b, both_b[0], both_b[1], mask_b) + [hidden_b])
    three_chunks = spread(three_b, "section", 4)
    parts = input_back_narrow(idx, three_chunks, pieces)
    out_part = down_narrow_part(idx, after(three_chunks, parts), pieces)
    middle_grad = after(add_over_tensor(cot_own, parts), out_part)
    grad_chunks = spread(middle_grad, "tensor", 8)
    down_2, = into_vmem(after(down_wide, middle_grad))
    grad_chunks = after(grad_chunks, down_2)
    own, parts = hidden_grad_wide(idx, grad_chunks, down_2)

    received = send(parts, "section", 4)
    out_sum = lax.psum_scatter(after(out_part, own), "tensor", scatter_dimension=0, tiled=True)
    outputs = (mid_rows.astype(F32) + out_sum).astype(BF)

    gate_2, = into_vmem(after(gate_wide, own))
    dhid_a = add_up(own, after(received, gate_2))
    pair_a = jnp.stack(grads_of(dhid_a, both_a[0], both_a[1], mask_a))
    up_2, = into_vmem(after(up_wide, dhid_a))
    pair_chunks = after(spread(pair_a, "section", 4), up_2)
    input_grad = add_over_tensor(middle_grad, input_back_wide(idx, pair_chunks, gate_2, up_2))
    return (
        outputs.reshape(1, quarter, outputs.shape[1]),
        input_grad.reshape(blocks, quarter, width),
    )


def solution(mesh):
    in_specs = (
        P(None, "dp", ("section", "tensor")),
        P("section", "tensor"),
        P("section", "tensor"),
        P("tensor", "section"),
        P(),
        P(("section", "tensor"), "dp"),
        P(("section", "tensor"), "dp"),
        P("dp", ("section", "tensor")),
        P(),
        P("tensor", "dp", "section"),
    )
    out_specs = (P("tensor", "dp", "section"), P(None, "dp", ("section", "tensor")))
    return jax.shard_map(body, mesh=mesh, in_specs=in_specs, out_specs=out_specs, check_vma=False)
```

```python
import jax
import jax.numpy as jnp
from jax import lax
from jax.experimental import pallas as pl
from jax.experimental.pallas import tpu as pltpu
from jax.sharding import PartitionSpec as P

BF = jnp.bfloat16
F32 = jnp.float32
VMEM = 8 << 20
NT = (((1,), (1,)), ((), ()))


def ring(n, shift):
    return [(i, (i + shift) % n) for i in range(n)]


def send(parts, axis, n):
    return [lax.ppermute(p, axis, ring(n, r)) for r, p in zip(range(1, n), parts)]


def spread(own, axis, n):
    return [own] + send([own] * (n - 1), axis, n)


VM = pl.BlockSpec(memory_space=pltpu.VMEM)
SM = pl.BlockSpec(memory_space=pltpu.SMEM)


def fill_features(scratch, refs, t, mix, slot):
    width = refs[0].shape[1]
    for k, ref in enumerate(refs):
        owner = lax.rem(t - k + 8, 8)
        at = pl.multiple_of(slot(owner, mix) * width, width)
        scratch[:, pl.ds(at, width)] = ref[...]


def fill_rows(scratch, refs, me, n):
    rows = refs[0].shape[-2]
    for k, ref in enumerate(refs):
        at = pl.multiple_of(lax.rem(me - k + n, n) * rows, rows)
        if len(ref.shape) == 3:
            for g in range(2):
                scratch[g, pl.ds(at, rows), :] = ref[g]
        else:
            scratch[pl.ds(at, rows), :] = ref[...]


def plain_slot(owner, mix):
    return owner


def narrow_slot(owner, mix):
    return (((owner & 1) << 2) | (owner >> 1)) ^ mix


def narrow_owner(slot, mix):
    swapped = slot ^ mix
    return ((swapped & 3) << 1) | (swapped >> 2)


def call(kernel, idx, operands, outs, scratch, flops, moved):
    return pl.pallas_call(
        kernel,
        in_specs=[SM] + [VM] * len(operands),
        out_specs=[VM] * len(outs),
        out_shape=[pltpu.VMEM(shape, kind) for shape, kind in outs],
        scratch_shapes=scratch,
        compiler_params=pltpu.CompilerParams(vmem_limit_bytes=VMEM),
        cost_estimate=pl.CostEstimate(flops=flops, bytes_accessed=moved, transcendentals=0),
    )(idx, *operands)


def into_vmem(*weights):
    n = len(weights)

    def kernel(*refs):
        copies = [
            pltpu.make_async_copy(refs[i], refs[n + i], refs[2 * n].at[i]) for i in range(n)
        ]
        for c in copies:
            c.start()
        for c in copies:
            c.wait()

    moved = sum(w.size * 2 for w in weights)
    return pl.pallas_call(
        kernel,
        in_specs=[pl.BlockSpec(memory_space=pltpu.HBM)] * n,
        out_specs=[VM] * n,
        out_shape=[pltpu.VMEM(w.shape, w.dtype) for w in weights],
        scratch_shapes=[pltpu.SemaphoreType.DMA((n,))],
        compiler_params=pltpu.CompilerParams(vmem_limit_bytes=1 << 20),
        cost_estimate=pl.CostEstimate(flops=0, bytes_accessed=2 * moved, transcendentals=0),
    )(*weights)


def gate_up(idx, chunks, weights, narrow):
    tokens, width = chunks[0].shape
    feats = 8 * width
    units = weights[0].shape[-1]
    block = 256
    rows = tokens // 4
    mid_rows = tokens // 8
    n_w = len(weights)

    def kernel(idx_ref, *refs):
        xs, ws = refs[:8], refs[8 : 8 + n_w]
        outs = refs[8 + n_w : 12 + n_w]
        mid, lhs, val = refs[12 + n_w :]
        s, t, mix = idx_ref[0], idx_ref[1], idx_ref[2]
        fill_features(lhs, xs, t, mix, narrow_slot if narrow else plain_slot)
        if narrow:
            row = pl.multiple_of(t * mid_rows, mid_rows)
            for k, ref in enumerate(xs):
                owner = lax.rem(t - k + 8, 8)
                to = pl.multiple_of(owner * width, width)
                mid[:, pl.ds(to, width)] = ref[pl.ds(row, mid_rows), :]
        for g in range(2):
            for at in range(0, units, block):
                size = min(block, units - at)
                if narrow:
                    value = None
                    for j, w in enumerate(ws):
                        term = jnp.dot(
                            lhs[:, j * width : (j + 1) * width],
                            w[g, :, at : at + size],
                            preferred_element_type=F32,
                        )
                        value = term if value is None else value + term
                else:
                    value = jnp.dot(lhs[...], ws[g][:, at : at + size], preferred_element_type=F32)
                val[:, :size] = value
                for r, out in enumerate(outs):
                    row = pl.multiple_of(lax.rem(s + r, 4) * rows, rows)
                    out[g, :, at : at + size] = val[pl.ds(row, rows), :size].astype(out.dtype)

    res = call(
        kernel,
        idx,
        (*chunks, *weights),
        [((2, rows, units), F32)] + [((2, rows, units), BF)] * 3 + [((mid_rows, feats), BF)],
        [pltpu.VMEM((tokens, feats), BF), pltpu.VMEM((tokens, block), F32)],
        4 * tokens * feats * units,
        4 * feats * units,
    )
    return res[0], res[1:4], res[4]


def down_wide_part(idx, chunks, down_w):
    rows, units = chunks[0].shape
    tokens = 4 * rows
    feats = down_w.shape[1]
    width = feats // 8

    def kernel(idx_ref, *refs):
        hs, w, out, lhs = refs[:4], refs[4], refs[5], refs[6]
        fill_rows(lhs, hs, idx_ref[0], 4)
        for k in range(8):
            out[k] = jnp.dot(
                lhs[...], w[:, k * width : (k + 1) * width], preferred_element_type=F32
            ).astype(BF)

    return call(
        kernel,
        idx,
        (*chunks, down_w),
        [((8, tokens, width), BF)],
        [pltpu.VMEM((tokens, units), BF)],
        2 * tokens * feats * units,
        2 * feats * units,
    )[0]


def down_narrow_part(idx, chunks, weights):
    _, rows, units = chunks[0].shape
    tokens = 4 * rows
    width = weights[0].shape[1]
    feats = 8 * width

    def kernel(idx_ref, *refs):
        hs, ws, out, lhs = refs[:4], refs[4:12], refs[12], refs[13]
        mix = idx_ref[2]
        for k, h in enumerate(hs):
            row = pl.multiple_of(lax.rem(idx_ref[0] - k + 4, 4) * rows, rows)
            lhs[pl.ds(row, rows), :] = h[2]
        for j, w in enumerate(ws):
            at = pl.multiple_of(narrow_owner(j, mix) * width, width)
            out[:, pl.ds(at, width)] = lax.dot_general(
                lhs[...], w[2], NT, preferred_element_type=F32
            )

    return call(
        kernel,
        idx,
        (*chunks, *weights),
        [((tokens, feats), F32)],
        [pltpu.VMEM((tokens, units), BF)],
        2 * tokens * feats * units,
        2 * feats * units,
    )[0]


def hidden_grad_wide(idx, chunks, down_w):
    tokens, width = chunks[0].shape
    feats = 8 * width
    units = down_w.shape[0]
    block = 256
    rows = tokens // 4

    def kernel(idx_ref, *refs):
        xs, w, outs, lhs, val = refs[:8], refs[8], refs[9:13], refs[13], refs[14]
        s, t = idx_ref[0], idx_ref[1]
        fill_features(lhs, xs, t, 0, plain_slot)
        for at in range(0, units, block):
            val[...] = lax.dot_general(
                lhs[...], w[at : at + block, :], NT, preferred_element_type=F32
            )
            for r, out in enumerate(outs):
                row = pl.multiple_of(lax.rem(s + r, 4) * rows, rows)
                out[:, at : at + block] = val[pl.ds(row, rows), :].astype(out.dtype)

    res = call(
        kernel,
        idx,
        (*chunks, down_w),
        [((rows, units), F32)] + [((rows, units), BF)] * 3,
        [pltpu.VMEM((tokens, feats), BF), pltpu.VMEM((tokens, block), F32)],
        2 * tokens * feats * units,
        2 * feats * units,
    )
    return res[0], res[1:]


def hidden_grad_narrow(idx, cot, weights):
    tokens, feats = cot.shape
    width = feats // 8
    units = weights[0].shape[2]
    block = 256
    rows = tokens // 4

    def kernel(idx_ref, *refs):
        lhs, ws, outs = refs[0], refs[1:9], refs[9:13]
        own, val = refs[13:]
        s, t, mix = idx_ref[0], idx_ref[1], idx_ref[2]
        own[...] = lhs[:, pl.ds(pl.multiple_of(t * width, width), width)]
        for at in range(0, units, block):
            size = min(block, units - at)
            total = None
            for j, w in enumerate(ws):
                left = lhs[:, pl.ds(pl.multiple_of(narrow_owner(j, mix) * width, width), width)]
                term = jnp.dot(left, w[2, :, at : at + size], preferred_element_type=F32)
                total = term if total is None else total + term
            val[:, :size] = total
            for r, out in enumerate(outs):
                row = pl.multiple_of(lax.rem(s + r, 4) * rows, rows)
                out[:, at : at + size] = val[pl.ds(row, rows), :size].astype(out.dtype)

    res = call(
        kernel,
        idx,
        (cot, *weights),
        [((rows, units), F32)] + [((rows, units), BF)] * 3 + [((tokens, width), BF)],
        [pltpu.VMEM((tokens, block), F32)],
        2 * tokens * feats * units,
        2 * feats * units,
    )
    return res[0], res[1:4], res[4]


def input_back_wide(idx, chunks, gate_w, up_w):
    _, rows, units = chunks[0].shape
    tokens = 4 * rows
    width = gate_w.shape[0] // 8
    feats = 8 * width

    def kernel(idx_ref, *refs):
        ps, g, u, out, lhs = refs[:4], refs[4], refs[5], refs[6], refs[7]
        fill_rows(lhs, ps, idx_ref[0], 4)
        for k in range(8):
            rows_k = slice(k * width, (k + 1) * width)
            value = lax.dot_general(lhs[0], g[rows_k, :], NT, preferred_element_type=F32)
            value += lax.dot_general(lhs[1], u[rows_k, :], NT, preferred_element_type=F32)
            out[k] = value.astype(BF)

    return call(
        kernel,
        idx,
        (*chunks, gate_w, up_w),
        [((8, tokens, width), BF)],
        [pltpu.VMEM((2, tokens, units), BF)],
        4 * tokens * feats * units,
        4 * feats * units,
    )[0]


def input_back_narrow(idx, chunks, weights):
    _, rows, units = chunks[0].shape
    tokens = 4 * rows
    width = weights[0].shape[1]
    feats = 8 * width

    def kernel(idx_ref, *refs):
        ps, ws, out, lhs = refs[:4], refs[4:12], refs[12], refs[13]
        mix = idx_ref[2]
        fill_rows(lhs, ps, idx_ref[0], 4)
        for j, w in enumerate(ws):
            value = lax.dot_general(lhs[0], w[0], NT, preferred_element_type=F32)
            value += lax.dot_general(lhs[1], w[1], NT, preferred_element_type=F32)
            out[narrow_owner(j, mix)] = value.astype(BF)

    return call(
        kernel,
        idx,
        (*chunks, *weights),
        [((8, tokens, width), BF)],
        [pltpu.VMEM((2, tokens, units), BF)],
        4 * tokens * feats * units,
        4 * feats * units,
    )[0]


def add_up(own, received):
    total = own
    for r in received:
        total = total + r.astype(F32)
    return total


def add_over_tensor(base, parts):
    received = lax.all_to_all(parts, "tensor", split_axis=0, concat_axis=0, tiled=True)
    return (base.astype(F32) + jnp.sum(received.astype(F32), axis=0)).astype(BF)


def hidden_of(gate, upper, mask):
    sigma = jax.nn.sigmoid(gate)
    return (gate * sigma * upper * mask).astype(BF)


def grads_of(dhid, gate, upper, mask):
    sigma = jax.nn.sigmoid(gate)
    dgate = (dhid * upper * sigma * (1.0 + gate * (1.0 - sigma)) * mask).astype(BF)
    dup = (dhid * gate * sigma * mask).astype(BF)
    return [dgate, dup]


def after(value, *earlier):
    return lax.optimization_barrier((value, earlier))[0]


CORES = [(0, 1), (1, 0), (2, 3), (3, 2)]


def own_halves(idx, gate_w, up_w, down_w):
    width, units = gate_w.shape
    size = units // 2

    def kernel(idx_ref, g, u, d, *outs):
        bit = (idx_ref[1] >> 1) & 1
        for j, out in enumerate(outs):
            at = pl.multiple_of((bit ^ j) * size, size)
            out[0] = g[:, pl.ds(at, size)]
            out[1] = u[:, pl.ds(at, size)]
            out[2] = d[pl.ds(at, size), :].T

    return call(
        kernel,
        idx,
        (gate_w, up_w, down_w),
        [((3, width, size), BF)] * 2,
        [],
        0,
        12 * width * units,
    )


def hand_out(piece, flip_x, flip_half):
    perm = []
    for d in range(4):
        for t in range(8):
            g, a, b = t >> 2, (t >> 1) & 1, t & 1
            to_d = (g ^ flip_x) * 2 + b
            to_t = 4 * (d & 1) + 2 * (d >> 1) + (a ^ flip_half)
            perm.append((d * 8 + t, to_d * 8 + to_t))
    return lax.ppermute(piece, ("dp", "tensor"), perm)


def to_sibling(pieces):
    return [lax.ppermute(p, "dp", CORES) for p in pieces]


def body(
    inputs,
    gate_wide,
    up_wide,
    down_wide,
    width_wide,
    gate_narrow,
    up_narrow,
    down_narrow,
    width_narrow,
    cotangent,
):
    section = lax.axis_index("section").astype(jnp.int32)
    tensor = lax.axis_index("tensor").astype(jnp.int32)
    dp = lax.axis_index("dp").astype(jnp.int32)
    mix = (dp & 1) * 4 + (dp >> 1) * 2 + (tensor & 1)
    idx = jnp.stack([section, tensor, mix])
    units_a = gate_wide.shape[1]
    units_b = gate_narrow.shape[1] // 2
    mask_a = (
        tensor * units_a + jnp.arange(units_a, dtype=jnp.int32) < width_wide[0]
    ).astype(F32)
    from_dp = 2 * ((tensor >> 1) & 1) + (tensor >> 2)
    mask_b = (
        (2 * from_dp + (tensor & 1)) * units_b + jnp.arange(units_b, dtype=jnp.int32) < width_narrow[0]
    ).astype(F32)
    blocks, quarter, width = inputs.shape
    tokens = blocks * quarter
    own_in = inputs.reshape(tokens, width)

    half = own_halves(idx, gate_narrow, up_narrow, down_narrow)
    cot_rows = lax.all_gather(cotangent[0], "tensor", axis=0, tiled=True)
    x_chunks = spread(own_in, "tensor", 8)
    gate_1, up_1 = into_vmem(*after((gate_wide, up_wide), x_chunks[1], x_chunks[2]))
    x_chunks = after(x_chunks, half)
    ready = after(half, x_chunks)
    a00, a11 = hand_out(ready[0], 0, 0), hand_out(ready[1], 1, 1)
    ready = after(half, (a00, a11))
    a01, a10 = hand_out(ready[1], 0, 1), hand_out(ready[0], 1, 0)

    own, parts, _ = gate_up(idx, x_chunks, (gate_1, up_1), False)
    down_1, = into_vmem(after(down_wide, own))
    both_a = add_up(own, send(parts, "section", 4))
    hidden_a = after(hidden_of(both_a[0], both_a[1], mask_a), (a00, a11))
    hidden_chunks = after(spread(hidden_a, "section", 4), down_1)
    s00, s11 = to_sibling(after([a00, a11], hidden_chunks))
    parts = after(down_wide_part(idx, hidden_chunks, down_1), (a01, a10))
    middle = add_over_tensor(own_in, parts)
    middle = after(middle, cot_rows)
    s01, s10 = to_sibling(after([a01, a10], middle))
    pieces = [a00, a01, a10, a11, s00, s01, s10, s11]
    mid_chunks = spread(middle, "tensor", 8)
    own, parts, cot_own = hidden_grad_narrow(idx, cot_rows, pieces)
    dhid_b = add_up(own, send(parts, "section", 4))
    mid_chunks = after(mid_chunks, cot_own)
    own, parts, mid_rows = gate_up(idx, mid_chunks, pieces, True)
    both_b = add_up(own, send(parts, "section", 4))

    hidden_b = hidden_of(both_b[0], both_b[1], mask_b)
    three_b = jnp.stack(grads_of(dhid_b, both_b[0], both_b[1], mask_b) + [hidden_b])
    three_chunks = spread(three_b, "section", 4)
    parts = input_back_narrow(idx, three_chunks, pieces)
    out_part = down_narrow_part(idx, after(three_chunks, parts), pieces)
    middle_grad = after(add_over_tensor(cot_own, parts), out_part)
    grad_chunks = spread(middle_grad, "tensor", 8)
    down_2, = into_vmem(after(down_wide, middle_grad))
    grad_chunks = after(grad_chunks, down_2)
    own, parts = hidden_grad_wide(idx, grad_chunks, down_2)

    received = send(parts, "section", 4)
    out_sum = lax.psum_scatter(after(out_part, middle_grad), "tensor", scatter_dimension=0, tiled=True)
    outputs = (mid_rows.astype(F32) + out_sum).astype(BF)

    gate_2, = into_vmem(after(gate_wide, own))
    dhid_a = add_up(own, after(received, gate_2))
    pair_a = jnp.stack(grads_of(dhid_a, both_a[0], both_a[1], mask_a))
    up_2, = into_vmem(after(up_wide, dhid_a))
    pair_chunks = after(spread(pair_a, "section", 4), up_2)
    input_grad = add_over_tensor(middle_grad, input_back_wide(idx, pair_chunks, gate_2, up_2))
    return (
        outputs.reshape(1, quarter, outputs.shape[1]),
        input_grad.reshape(blocks, quarter, width),
    )


def solution(mesh):
    in_specs = (
        P(None, "dp", ("section", "tensor")),
        P("section", "tensor"),
        P("section", "tensor"),
        P("tensor", "section"),
        P(),
        P(("section", "tensor"), "dp"),
        P(("section", "tensor"), "dp"),
        P("dp", ("section", "tensor")),
        P(),
        P("tensor", "dp", "section"),
    )
    out_specs = (P("tensor", "dp", "section"), P(None, "dp", ("section", "tensor")))
    return jax.shard_map(body, mesh=mesh, in_specs=in_specs, out_specs=out_specs, check_vma=False)
```
